256 devices in a mesh: section: 4 (over y), vocab: 32 (over x, z), dp: 2 (over core).
Axes of the slice: x: 4, y: 4, z: 8, core: 2. Of those that a mesh axis runs over, the one named last changes fastest.
Arguments:
- student_hidden: bfloat16 [2, 256, 3584], P('dp', ('section', 'vocab')), may hold values from -6 to 6
- teacher_hidden: bfloat16 [2, 256, 4608], P('dp', 'section'), may hold values from -6 to 6
- student_gain: float32 [3584], replicated, may hold values from 0.5 to 1.5
- teacher_gain: float32 [4608], replicated, may hold values from 0.5 to 1.5
- student_head: bfloat16 [3584, 131072], P('dp', ('section', 'vocab')), may hold values from -0.3125 to 0.3125
- teacher_head: bfloat16 [4608, 131072], P('dp', ('section', 'vocab')), may hold values from -0.25 to 0.25
- targets: int32 [2, 256], P('dp'), may hold values from 0 to 131071
Outputs:
- row_loss: float32 [2, 256], P('dp', ('section', 'vocab'))
- head_grad: bfloat16 [3584, 131072], P('dp', ('section', 'vocab'))
The draws below stay inside these ranges and needn't reach their ends.
All inputs are finite; a program needn't handle non-finite values.
Results may differ from the reference program's by a relative error of at most 0.025.
Values may be sent and summed in bfloat16 or wider, within the bound.
No kernel may reach another device: no remote copies, remote signals or barrier semaphores. Data moves between devices by JAX's collectives and lax.ppermute only.
A program may use at most 128 MiB of HBM per device.

```python
import math
import jax
import jax.numpy as jnp
import numpy as np
from jax import lax

D_S = 3584
D_T = 4608
ROWS = 256
VOCAB = 131072
N_DP = 2


def set_ends(entries, key, smallest, high):
    index_at = [jax.random.randint(jax.random.fold_in(key, axis), (), 0, length) for axis, length in enumerate(entries.shape)]
    main_axis = entries.shape.index(max(entries.shape))
    next_to = index_at[:main_axis] + [(index_at[main_axis] + 1) % entries.shape[main_axis]] + index_at[main_axis + 1:]
    return entries.at[tuple(index_at)].set(smallest).at[tuple(next_to)].set(high)


def shard_levels(own_key, extent, cuts, smallest, high):
    level, own = 1.0, jax.random.fold_in(own_key, 6)
    for position, shards_of in cuts:
        heights = jnp.exp(jax.random.uniform(jax.random.fold_in(own, position), (shards_of,), jnp.float32, smallest / len(cuts), high / len(cuts)))
        level = level * jnp.repeat(heights, extent[position] // shards_of).reshape([-1 if axis == position else 1 for axis in range(len(extent))])
    return level


def ranked_wide(key, extent, count, slope):
    weights = [min(1 << octave, count + 1 - (1 << octave)) * (1 << 20) // math.isqrt((1 << octave) ** slope) + 1 for octave in range((count + 1).bit_length()) if 1 << octave <= count]
    width = 1 + sum(weights) // (1 << 30)
    listing = np.cumsum(np.array([max(1, weight // width) for weight in weights]))
    ticket = jax.random.randint(jax.random.fold_in(key, 1), extent, 0, int(listing[len(weights) - 1]))
    start = jnp.left_shift(1, jnp.searchsorted(jnp.asarray(listing, jnp.int32), ticket, side="right").astype(jnp.int32))
    rank = start - 1 + jax.random.randint(jax.random.fold_in(key, 4), extent, 0, 1 << 30) % jnp.minimum(start, count + 1 - start)
    return jax.random.permutation(jax.random.fold_in(key, 2), count)[rank].astype(jnp.int32)


def gaussian(key, extent, scale, reach, shards=(), held_as=jnp.bfloat16):
    result = jax.random.normal(key, extent, jnp.float32) * scale
    if len(shards) > 0:
        result = shard_levels(key, extent, shards, -0.22, 0.18) * result
    return jnp.clip(result, min=-reach, max=reach).astype(held_as)


def setup_inputs(seed: int = 0) -> dict:
    streams_of = jax.random.split(jax.random.key(seed), 8)
    student_hidden = gaussian(streams_of[0], (N_DP, ROWS, D_S), 1.0, 6.0, ((0, 2), (1, 128)))
    teacher_hidden = gaussian(streams_of[1], (N_DP, ROWS, D_T), 1.0, 6.0, ((0, 2), (1, 4)))
    student_gain = jnp.clip(1.0 + 0.1 * jax.random.normal(streams_of[2], (D_S,), jnp.float32), 0.5, 1.5)
    teacher_gain = jnp.clip(1.0 + 0.1 * jax.random.normal(streams_of[3], (D_T,), jnp.float32), 0.5, 1.5)
    student_head = gaussian(streams_of[4], (D_S, VOCAB), (D_S // 9) ** -0.5, 0.3125, ((0, 2), (1, 128)))
    teacher_head = gaussian(streams_of[5], (D_T, VOCAB), (D_T // 9) ** -0.5, 0.25, ((0, 2), (1, 128)))
    targets = set_ends(ranked_wide(streams_of[6], (N_DP, ROWS), VOCAB, 2), jax.random.fold_in(streams_of[6], 3), 0, VOCAB - 1).astype(jnp.int32)
    return {"student_hidden": student_hidden, "teacher_hidden": teacher_hidden, "student_gain": student_gain, "teacher_gain": teacher_gain, "student_head": student_head, "teacher_head": teacher_head, "targets": targets}


def rms_norm(hidden, scales):
    values = hidden.astype(jnp.float32)
    spread = lax.optimization_barrier(jnp.mean(values * values, axis=-1, keepdims=True))
    return (values * lax.rsqrt(spread + 1e-06) * scales).astype(jnp.bfloat16)

def soft_cap(logits):
    return (30.0 * jnp.tanh(logits / 30.0)).astype(jnp.bfloat16)

def reference(student_hidden, teacher_hidden, student_gain, teacher_gain, student_head, teacher_head, targets):
    normed_student = rms_norm(student_hidden.reshape(N_DP * ROWS, D_S), student_gain)
    normed_teacher = rms_norm(teacher_hidden.reshape(N_DP * ROWS, D_T), teacher_gain)
    stud_vals = soft_cap(jnp.dot(normed_student, student_head, preferred_element_type=jnp.float32)).astype(jnp.float32)
    teach_vals = soft_cap(jnp.dot(normed_teacher, teacher_head, preferred_element_type=jnp.float32)).astype(jnp.float32)
    target_hit = (lax.broadcasted_iota(jnp.int32, stud_vals.shape, 1) == targets.reshape(N_DP * ROWS, 1)).astype(jnp.float32)
    teach_exp = jnp.exp(teach_vals)
    stud_exp = jnp.exp(stud_vals)
    teach_total = lax.optimization_barrier(jnp.sum(teach_exp, axis=1))
    stud_total = lax.optimization_barrier(jnp.sum(stud_exp, axis=1))
    cross_sum = lax.optimization_barrier(jnp.sum(teach_exp * (teach_vals - stud_vals), axis=1))
    target_logit = lax.optimization_barrier(jnp.sum(target_hit * stud_vals, axis=1))
    row_loss = cross_sum / teach_total - jnp.log(teach_total) + 2.0 * jnp.log(stud_total) - target_logit
    row_grad = ((2.0 * stud_exp / stud_total[:, None] - teach_exp / teach_total[:, None] - target_hit) * (1.0 - stud_vals * stud_vals / 900.0)).astype(jnp.bfloat16)
    head_grad = lax.dot_general(normed_student, row_grad, (((0,), (0,)), ((), ())), preferred_element_type=jnp.float32).astype(jnp.bfloat16)
    return (row_loss.reshape(N_DP, ROWS), head_grad)
```

```python
import jax
import jax.numpy as jnp
from jax import lax
from jax.sharding import Mesh, PartitionSpec as P

F32 = jnp.float32
BF16 = jnp.bfloat16


def rms_norm(hidden, scales):
    values = hidden.astype(F32)
    spread = jnp.mean(values * values, axis=-1, keepdims=True)
    return (values * lax.rsqrt(spread + 1e-06) * scales).astype(BF16)


def soft_cap(logits):
    return (30.0 * jnp.tanh(logits / 30.0)).astype(BF16)


def up(n, k):
    return [(i, (i + k) % n) for i in range(n)]


def swap_cores(value):
    return lax.ppermute(value, "c", [(0, 1), (1, 0)])


def mine_and_other(first, second, core):
    return jnp.where(core == 0, first, second), jnp.where(core == 0, second, first)


def ring(block, axis, n):
    blocks = [block]
    from_low = from_high = block
    for _ in range(n // 2 - 1):
        from_low = lax.ppermute(from_low, axis, up(n, 1))
        from_high = lax.ppermute(from_high, axis, up(n, -1))
        blocks += [from_low, from_high]
    half = block.shape[0] // 2
    blocks.append(
        jnp.concatenate(
            [
                lax.ppermute(from_low[:half], axis, up(n, 1)),
                lax.ppermute(from_high[half:], axis, up(n, -1)),
            ]
        )
    )
    return blocks


def ring_order(n):
    order = [0]
    for step in range(1, n // 2):
        order += [n - step, step]
    return order + [n // 2]


def by_distance(entries, n):
    order = ring_order(n)
    return [entries[order.index(d)] for d in range(n)]


def turn(array, amount):
    n = array.shape[0]
    return lax.dynamic_slice_in_dim(jnp.concatenate([array, array]), amount % n, n)


def dot(left, right):
    return jnp.dot(left, right, preferred_element_type=F32)


def shards(
    student_hidden, teacher_hidden, student_gain, teacher_gain, student_head, teacher_head, targets
):
    nx, ny, nz = lax.axis_size("x"), lax.axis_size("y"), lax.axis_size("z")
    x, y, z, core = (lax.axis_index(a) for a in ("x", "y", "z", "c"))
    rows = student_hidden.shape[1]
    k_s, vocab = student_head.shape
    k_t = teacher_head.shape[0]
    per_plane = ny * nx * rows

    normed = rms_norm(student_hidden[0], student_gain)
    halves = normed.reshape(rows, 2, k_s).transpose(1, 0, 2)
    sent = jnp.broadcast_to(halves[None], (ny * nx, 2, rows, k_s)).reshape(ny * nx * 2, rows, k_s)
    got = lax.all_to_all(sent, ("y", "x", "c"), 0, 0, tiled=True).reshape(ny * nx, 2, rows, k_s)
    own, other = mine_and_other(got[:, 0], got[:, 1], core)
    plane = jnp.concatenate([own.reshape(per_plane, k_s), other.reshape(per_plane, k_s)])
    planes = by_distance(ring(plane, "z", nz), nz)

    t_norm = rms_norm(teacher_hidden[0], teacher_gain)
    section = t_norm.shape[0]
    t_norm = t_norm.reshape(nx, nz, rows, 2 * k_t).transpose(1, 0, 2, 3)
    t_norm = turn(t_norm, z).reshape(section, 2, k_t)
    t_keep, t_send = mine_and_other(t_norm[:, 0], t_norm[:, 1], core)
    t_block = jnp.concatenate([t_keep, swap_cores(t_send)])
    t_blocks = by_distance(ring(t_block, "y", ny), ny)

    t_all = jnp.stack(t_blocks).reshape(ny, 2, section, k_t)
    t_part = dot(t_all.transpose(1, 0, 2, 3).reshape(2 * ny * section, k_t), teacher_head)
    half_rows = ny * section
    t_logits = t_part[:half_rows] + swap_cores(t_part[half_rows:])
    capped_teacher = soft_cap(t_logits).reshape(ny, nz, nx * rows, vocab)
    capped_teacher = turn(capped_teacher, -y).transpose(1, 0, 2, 3).reshape(half_rows, vocab)

    s_rows = jnp.stack(planes).reshape(nz, 2, per_plane, k_s).transpose(1, 0, 2, 3)
    s_rows = s_rows.reshape(2 * half_rows, k_s)
    s_part = dot(s_rows, student_head)
    s_logits = s_part[:half_rows] + swap_cores(s_part[half_rows:])
    capped_student = soft_cap(s_logits)

    stud_vals = capped_student.astype(F32)
    teach_vals = capped_teacher.astype(F32)
    ordered = targets[0].reshape(ny, nx, nz, rows).transpose(2, 0, 1, 3)
    first = ((y * nx + x) * nz + z) * vocab
    local_targets = turn(ordered, z).reshape(half_rows) - first
    hit = (lax.broadcasted_iota(jnp.int32, stud_vals.shape, 1) == local_targets[:, None]).astype(F32)
    teach_exp = jnp.exp(teach_vals)
    stud_exp = jnp.exp(stud_vals)
    sums = jnp.stack(
        [
            jnp.sum(teach_exp, axis=1),
            jnp.sum(stud_exp, axis=1),
            jnp.sum(teach_exp * (teach_vals - stud_vals), axis=1),
            jnp.sum(hit * stud_vals, axis=1),
        ]
    ).reshape(4, nz, per_plane)
    sums = sums.transpose(1, 0, 2).reshape(nz, 4 * per_plane)
    spread = jnp.broadcast_to(sums[None], (ny * nx,) + sums.shape)
    sums = jnp.sum(lax.all_to_all(spread, ("y", "x"), 0, 0, tiled=True), axis=0)
    sums = turn(sums, -z)
    spread = jnp.broadcast_to(sums[None], (nz,) + sums.shape)
    sums = jnp.sum(lax.all_to_all(spread, "z", 0, 0, tiled=True), axis=0)
    sums = turn(sums, z).reshape(nz, 4, per_plane)
    teach_total, stud_total, cross_sum, target_logit = (
        sums[:, q].reshape(half_rows) for q in range(4)
    )
    here = sums[0].reshape(4, ny * nx, rows)
    tt, st, cs, tl = (lax.dynamic_index_in_dim(here[q], y * nx + x, 0, False) for q in range(4))
    row_loss = (cs / tt - jnp.log(tt) + 2.0 * jnp.log(st) - tl)[None, :]

    scaled = 2.0 * stud_exp / stud_total[:, None] - teach_exp / teach_total[:, None] - hit
    row_grad = (scaled * (1.0 - stud_vals * stud_vals / 900.0)).astype(BF16)
    both = jnp.concatenate([row_grad, swap_cores(row_grad)])
    head_grad = lax.dot_general(
        s_rows, both, (((0,), (0,)), ((), ())), preferred_element_type=F32
    ).astype(BF16)
    return (row_loss, head_grad)


def solution(mesh):
    sizes = mesh.shape
    cube = mesh.devices.reshape(sizes["section"], 4, sizes["vocab"] // 4, sizes["dp"])
    grid = Mesh(cube, ("y", "x", "z", "c"))
    group = ("y", "x", "z")
    placed = (
        P("c", group, None),
        P("c", "y", None),
        P(),
        P(),
        P("c", group),
        P("c", group),
        P("c", None),
    )
    return jax.shard_map(
        shards,
        mesh=grid,
        in_specs=placed,
        out_specs=(P("c", group), P("c", group)),
        check_vma=False,
    )
```

```python
import functools

import jax
import jax.numpy as jnp
from jax import lax
from jax.experimental import pallas as pl
from jax.experimental.pallas import tpu as pltpu
from jax.sharding import Mesh, PartitionSpec as P

F32 = jnp.float32
BF16 = jnp.bfloat16
I32 = jnp.int32
NY, NX, NZ = 4, 4, 8
ROWS = 2
PLANE = NY * NX * ROWS
OWN = NZ * PLANE
EARLY = OWN - PLANE
LANES = 128
VMEM = pl.BlockSpec(memory_space=pltpu.VMEM)


def params():
    return pltpu.CompilerParams(vmem_limit_bytes=50 * 1024 * 1024)


def cost(flops, bytes_accessed, transcendentals=0):
    return pl.CostEstimate(
        flops=flops, bytes_accessed=bytes_accessed, transcendentals=transcendentals
    )


def up(n, k):
    return [(i, (i + k) % n) for i in range(n)]


def swap_cores(value):
    return lax.ppermute(value, "c", [(0, 1), (1, 0)])


def ring(block, axis, n):
    blocks = [block]
    from_low = from_high = block
    for _ in range(n // 2 - 1):
        from_low = lax.ppermute(from_low, axis, up(n, 1))
        from_high = lax.ppermute(from_high, axis, up(n, -1))
        blocks += [from_low, from_high]
    half = block.shape[0] // 2
    blocks.append(lax.ppermute(from_low[:half], axis, up(n, 1)))
    blocks.append(lax.ppermute(from_high[half:], axis, up(n, -1)))
    return blocks


def distance(position):
    return jnp.where(position % 2 == 1, NZ - (position + 1) // 2, position // 2)


def natural_row(row, z):
    position, inner = row // PLANE, row % PLANE
    y, x, i = inner // (NX * ROWS), inner // ROWS % NX, inner % ROWS
    return ((y * NX + x) * NZ + (z + distance(position)) % NZ) * ROWS + i


def iota(shape, axis):
    return lax.broadcasted_iota(I32, shape, axis)


def normalize(hidden, gain):
    values = hidden.astype(F32)
    spread = jnp.mean(values * values, axis=-1, keepdims=True)
    return (values * lax.rsqrt(spread + 1e-06) * gain).astype(BF16)


def student_norm_kernel(hidden_ref, gain_ref, out_ref):
    normed = normalize(hidden_ref[...], gain_ref[...])
    half = normed.shape[1] // 2
    for peer in range(NY * NX):
        out_ref[2 * peer] = normed[:, :half]
        out_ref[2 * peer + 1] = normed[:, half:]


def student_norm(hidden, gain):
    rows, width = hidden.shape
    return pl.pallas_call(
        student_norm_kernel,
        out_shape=jax.ShapeDtypeStruct((NY * NX * 2, rows, width // 2), BF16),
        in_specs=[VMEM, VMEM],
        out_specs=VMEM,
        compiler_params=params(),
    )(hidden, gain[None])


def teacher_norm_kernel(hidden_ref, gain_ref, keep_ref, send_ref):
    z, core = lax.axis_index("z"), lax.axis_index("c")
    normed = normalize(hidden_ref[...], gain_ref[...])
    n = normed.shape[0]
    row = iota((n, n), 0)
    position, x, i = row // (NX * ROWS), row // ROWS % NX, row % ROWS
    source = (x * NZ + (z + distance(position)) % NZ) * ROWS + i
    moved = jnp.where(iota((n, n), 1) == source, 1.0, 0.0).astype(BF16)
    normed = jnp.dot(moved, normed, preferred_element_type=F32).astype(BF16)
    half = normed.shape[1] // 2

    @pl.when(core == 0)
    def _():
        keep_ref[...] = normed[:, :half]
        send_ref[...] = normed[:, half:]

    @pl.when(core != 0)
    def _():
        keep_ref[...] = normed[:, half:]
        send_ref[...] = normed[:, :half]


def teacher_norm(hidden, gain):
    rows, width = hidden.shape
    part = jax.ShapeDtypeStruct((rows, width // 2), BF16)
    return pl.pallas_call(
        teacher_norm_kernel,
        out_shape=(part, part),
        in_specs=[VMEM, VMEM],
        out_specs=(VMEM, VMEM),
        compiler_params=params(),
    )(hidden, gain[None])


def teacher_logits_kernel(b0, b1, b2, b3, b4, w_ref, own_ref, other_ref, rows_ref):
    section = b0.shape[0] // 2

    @pl.when(pl.program_id(0) == 0)
    def _():
        y = lax.axis_index("y")
        row = iota((OWN, OWN), 0)
        position, inner = row // PLANE, row % PLANE
        apart = (inner // (NX * ROWS) - y) % NY
        place = jnp.where(
            apart == 0, 0, jnp.where(apart == NY - 1, 1, jnp.where(apart == 1, 2, 3))
        )
        source = place * section + position * (NX * ROWS) + inner % (NX * ROWS)
        moved = jnp.where(iota((OWN, OWN), 1) == source, 1.0, 0.0).astype(BF16)
        for side, last in ((0, b3), (1, b4)):
            part = pl.ds(side * section, section)
            whole = jnp.concatenate([b0[part], b1[part], b2[part], last[...]])
            rows_ref[pl.ds(side * OWN, OWN)] = jnp.dot(
                moved, whole, preferred_element_type=F32
            ).astype(BF16)

    result = jnp.dot(rows_ref[...], w_ref[...], preferred_element_type=F32)
    own_ref[...] = result[:OWN]
    other_ref[...] = result[OWN:]


def teacher_logits(blocks, head):
    k, vocab = head.shape
    tile = 256
    part = jax.ShapeDtypeStruct((OWN, vocab), F32)
    whole = [pl.BlockSpec(b.shape, lambda j: (0, 0)) for b in blocks]
    column = pl.BlockSpec((OWN, tile), lambda j: (0, j))
    return pl.pallas_call(
        teacher_logits_kernel,
        grid=(vocab // tile,),
        out_shape=(part, part),
        in_specs=whole + [pl.BlockSpec((k, tile), lambda j: (0, j))],
        out_specs=(column, column),
        scratch_shapes=[pltpu.VMEM((2 * OWN, k), BF16)],
        compiler_params=params(),
        cost_estimate=cost(4 * OWN * k * vocab, 2 * k * vocab + 8 * OWN * vocab),
    )(*blocks, head)


def student_logits_kernel(*refs):
    *blocks, w_ref, own_ref, other_ref, rows_ref = refs
    n = own_ref.shape[0]

    @pl.when(pl.program_id(0) == 0)
    def _():
        for q, block in enumerate(blocks):
            if len(blocks) == 2:
                rows_ref[pl.ds(q * PLANE, PLANE)] = block[...]
            else:
                rows_ref[pl.ds(q * PLANE, PLANE)] = block[:PLANE]
                rows_ref[pl.ds(n + q * PLANE, PLANE)] = block[PLANE:]

    result = jnp.dot(rows_ref[...], w_ref[...], preferred_element_type=F32)
    own_ref[...] = result[:n]
    other_ref[...] = result[n:]


def student_logits(blocks, head):
    k, vocab = head.shape
    tile = 256
    n = sum(b.shape[0] for b in blocks) // 2
    part = jax.ShapeDtypeStruct((n, vocab), F32)
    whole = [pl.BlockSpec(b.shape, lambda j: (0, 0)) for b in blocks]
    column = pl.BlockSpec((n, tile), lambda j: (0, j))
    return pl.pallas_call(
        student_logits_kernel,
        grid=(vocab // tile,),
        out_shape=(part, part),
        in_specs=whole + [pl.BlockSpec((k, tile), lambda j: (0, j))],
        out_specs=(column, column),
        scratch_shapes=[pltpu.VMEM((2 * n, k), BF16)],
        compiler_params=params(),
        cost_estimate=cost(4 * n * k * vocab, 2 * k * vocab + 8 * n * vocab),
    )(*blocks, head)


def soft_cap(logits):
    return (30.0 * jnp.tanh(logits / 30.0)).astype(BF16)


def local_targets(targets_ref, z, first, rows):
    shape = (rows.shape[0], OWN)
    here = iota(shape, 1) == natural_row(rows, z)
    return jnp.sum(jnp.where(here, targets_ref[...], 0), axis=1, keepdims=True) - first


def first_column(vocab):
    y, x, z = lax.axis_index("y"), lax.axis_index("x"), lax.axis_index("z")
    return ((y * NX + x) * NZ + z) * vocab


def fold(values):
    total = values[:, :LANES]
    for start in range(LANES, values.shape[1], LANES):
        total = total + values[:, start : start + LANES]
    return total


def vocab_sums(start, own, got, t_own, t_got, targets_ref, student_ref, teacher_ref, write):
    n, vocab = own.shape
    z, first = lax.axis_index("z"), first_column(vocab)
    step = 32
    for at in range(0, n, step):
        part, t_part = pl.ds(at, step), pl.ds(start + at, step)
        student = soft_cap(own[part] + got[part])
        teacher = soft_cap(t_own[t_part] + t_got[t_part])
        student_ref[part] = student
        teacher_ref[part] = teacher
        stud_vals, teach_vals = student.astype(F32), teacher.astype(F32)
        stud_exp, teach_exp = jnp.exp(stud_vals), jnp.exp(teach_vals)
        target = local_targets(targets_ref, z, first, iota((step, 1), 0) + (start + at))
        hit = iota((step, vocab), 1) == target
        write(0, at, fold(teach_exp))
        write(1, at, fold(stud_exp))
        write(2, at, fold(teach_exp * (teach_vals - stud_vals)))
        write(3, at, fold(jnp.where(hit, stud_vals, 0.0)))


def early_sums_kernel(own, got, t_own, t_got, targets_ref, student_ref, teacher_ref, sums_ref):
    def write(kind, at, value):
        sums_ref[kind, pl.ds(at, value.shape[0])] = value

    vocab_sums(0, own, got, t_own, t_got, targets_ref, student_ref, teacher_ref, write)


def early_sums(own, got, t_own, t_got, targets):
    n, vocab = own.shape
    values = jax.ShapeDtypeStruct((n, vocab), BF16)
    return pl.pallas_call(
        early_sums_kernel,
        out_shape=(values, values, jax.ShapeDtypeStruct((4, n, LANES), F32)),
        in_specs=[VMEM] * 5,
        out_specs=(VMEM,) * 3,
        compiler_params=params(),
        cost_estimate=cost(40 * n * vocab, 20 * n * vocab, 4 * n * vocab),
    )(own, got, t_own, t_got, targets)


def last_sums_kernel(
    own, got, t_own, t_got, targets_ref, early_ref, student_ref, teacher_ref, out_ref, sums_ref
):
    def write(kind, at, value):
        sums_ref[kind, pl.ds(EARLY + at, value.shape[0])] = value

    sums_ref[:, :EARLY] = early_ref[...]
    vocab_sums(EARLY, own, got, t_own, t_got, targets_ref, student_ref, teacher_ref, write)
    z = lax.axis_index("z")
    here = iota((OWN, OWN), 1) == natural_row(iota((OWN, OWN), 0), z)
    rows = []
    for kind in range(4):
        total = jnp.sum(sums_ref[kind], axis=1, keepdims=True)
        flat = jnp.sum(jnp.where(here, total, 0.0), axis=0, keepdims=True)
        rows += [flat[:, at : at + LANES] for at in range(0, OWN, LANES)]
    tile = jnp.concatenate(rows, axis=0)
    for peer in range(out_ref.shape[0]):
        out_ref[peer] = tile


def last_sums(own, got, t_own, t_got, targets, early):
    n, vocab = own.shape
    values = jax.ShapeDtypeStruct((n, vocab), BF16)
    return pl.pallas_call(
        last_sums_kernel,
        out_shape=(values, values, jax.ShapeDtypeStruct((NY * NX, 8, LANES), F32)),
        in_specs=[VMEM] * 6,
        out_specs=(VMEM,) * 3,
        scratch_shapes=[pltpu.VMEM((4, OWN, LANES), F32)],
        compiler_params=params(),
        cost_estimate=cost(40 * n * vocab, 20 * n * vocab, 4 * n * vocab),
    )(own, got, t_own, t_got, targets, early)


def gradient_kernel(*refs):
    (
        sums_ref,
        s_own0, s_own1, t_own0, t_own1,
        s_oth0, s_oth1, t_oth0, t_oth1,
        targets_ref, oth_targets_ref, *blocks, loss_ref, out_ref, rows_ref, grad_ref,
    ) = refs
    vocab = out_ref.shape[1]

    @pl.when(pl.program_id(0) == 0)
    def _():
        z, core = lax.axis_index("z"), lax.axis_index("c")
        first = first_column(vocab)
        position = (lax.axis_index("y") * NX + lax.axis_index("x")) * NZ + z
        here = iota((OWN, OWN), 1) == natural_row(iota((OWN, OWN), 0), z)
        totals = []
        for side in range(2):
            total = sums_ref[side]
            for peer in range(1, NZ):
                total = total + sums_ref[2 * peer + side]
            totals.append(total)
        own = jnp.where(core == 0, totals[0], totals[1])
        other = jnp.where(core == 0, totals[1], totals[0])

        def flat(tile, kind):
            return jnp.concatenate([tile[2 * kind : 2 * kind + 1], tile[2 * kind + 1 : 2 * kind + 2]], axis=1)

        teach_total, stud_total, cross_sum, target_logit = (flat(own, k) for k in range(4))
        loss = cross_sum / teach_total - jnp.log(teach_total) + 2.0 * jnp.log(stud_total) - target_logit
        lane = iota((1, OWN), 1)
        picked = [
            jnp.sum(jnp.where(lane == position * ROWS + i, loss, 0.0), axis=1, keepdims=True)
            for i in range(ROWS)
        ]
        loss_ref[...] = jnp.concatenate(picked, axis=1)

        for side, tile, s_refs, t_refs, targets in (
            (0, own, (s_own0, s_own1), (t_own0, t_own1), targets_ref),
            (1, other, (s_oth0, s_oth1), (t_oth0, t_oth1), oth_targets_ref),
        ):
            teach_scale = jnp.sum(jnp.where(here, 1.0 / flat(tile, 0), 0.0), axis=1, keepdims=True)
            stud_scale = jnp.sum(jnp.where(here, 2.0 / flat(tile, 1), 0.0), axis=1, keepdims=True)
            target = local_targets(targets, z, first, iota((OWN, 1), 0))
            step = 32
            for at in range(0, OWN, step):
                which, offset = (0, at) if at < EARLY else (1, at - EARLY)
                stud_vals = s_refs[which][pl.ds(offset, step)].astype(F32)
                teach_vals = t_refs[which][pl.ds(offset, step)].astype(F32)
                rows = slice(at, at + step)
                scaled = jnp.exp(stud_vals) * stud_scale[rows] - jnp.exp(teach_vals) * teach_scale[rows]
                hit = iota((step, vocab), 1) == target[rows]
                scaled = scaled - jnp.where(hit, 1.0, 0.0)
                value = scaled * (1.0 - stud_vals * stud_vals * (1.0 / 900.0))
                grad_ref[pl.ds(side * OWN + at, step)] = value.astype(BF16)
        for q, block in enumerate(blocks[: NZ - 1]):
            rows_ref[pl.ds(q * PLANE, PLANE)] = block[:PLANE]
            rows_ref[pl.ds(OWN + q * PLANE, PLANE)] = block[PLANE:]
        rows_ref[pl.ds(EARLY, PLANE)] = blocks[NZ - 1][...]
        rows_ref[pl.ds(OWN + EARLY, PLANE)] = blocks[NZ][...]

    tile = out_ref.shape[0]
    start = pl.multiple_of(pl.program_id(0) * tile, tile)
    out_ref[...] = lax.dot_general(
        rows_ref[:, pl.ds(start, tile)],
        grad_ref[...],
        (((0,), (0,)), ((), ())),
        preferred_element_type=F32,
    ).astype(BF16)


def gradient(sums, own, other, targets, oth_targets, blocks, k, vocab):
    tile = 256
    ops = [sums, *own, *other, targets, oth_targets, *blocks]
    in_specs = [pl.BlockSpec(a.shape, functools.partial(lambda n, j: (0,) * n, a.ndim)) for a in ops]
    return pl.pallas_call(
        gradient_kernel,
        grid=(k // tile,),
        out_shape=(
            jax.ShapeDtypeStruct((1, ROWS), F32),
            jax.ShapeDtypeStruct((k, vocab), BF16),
        ),
        in_specs=in_specs,
        out_specs=(
            pl.BlockSpec((1, ROWS), lambda j: (0, 0)),
            pl.BlockSpec((tile, vocab), lambda j: (j, 0)),
        ),
        scratch_shapes=[pltpu.VMEM((2 * OWN, k), BF16), pltpu.VMEM((2 * OWN, vocab), BF16)],
        compiler_params=params(),
        cost_estimate=cost(4 * OWN * k * vocab, 2 * k * vocab + 12 * OWN * vocab),
    )(*ops)


def shards(
    student_hidden, teacher_hidden, student_gain, teacher_gain, student_head, teacher_head, targets
):
    core = lax.axis_index("c")
    k_s, vocab = student_head.shape

    sent = student_norm(student_hidden[0], student_gain)
    got = lax.all_to_all(sent, ("y", "x", "c"), 0, 0, tiled=True)
    got = got.reshape(NY * NX, 2, ROWS, k_s)
    mine = jnp.where(core == 0, got[:, 0], got[:, 1]).reshape(PLANE, k_s)
    theirs = jnp.where(core == 0, got[:, 1], got[:, 0]).reshape(PLANE, k_s)
    planes = ring(jnp.concatenate([mine, theirs]), "z", NZ)

    keep, send = teacher_norm(teacher_hidden[0], teacher_gain)
    sections = ring(jnp.concatenate([keep, swap_cores(send)]), "y", NY)
    t_own, t_send = teacher_logits(sections, teacher_head)
    t_got = swap_cores(t_send)
    oth_targets = swap_cores(targets)

    s_own0, s_send0 = student_logits(planes[: NZ - 1], student_head)
    s_got0 = swap_cores(s_send0)
    stud0, teach0, early = early_sums(s_own0, s_got0, t_own, t_got, targets)
    s_own1, s_send1 = student_logits(planes[NZ - 1 :], student_head)
    s_got1 = swap_cores(s_send1)
    stud1, teach1, sums = last_sums(s_own1, s_got1, t_own, t_got, targets, early)
    own = (stud0, stud1, teach0, teach1)
    other = tuple(swap_cores(v) for v in own)
    sums = jnp.sum(lax.all_to_all(sums, ("y", "x"), 0, 0, tiled=True), axis=0)
    sums = jnp.broadcast_to(sums[None], (2 * NZ,) + sums.shape)
    sums = lax.all_to_all(sums, ("z", "c"), 0, 0, tiled=True)

    return gradient(sums, own, other, targets, oth_targets, planes, k_s, vocab)


def solution(mesh):
    cube = mesh.devices.reshape(NY, NX, NZ, 2)
    grid = Mesh(cube, ("y", "x", "z", "c"))
    group = ("y", "x", "z")
    placed = (
        P("c", group, None),
        P("c", "y", None),
        P(),
        P(),
        P("c", group),
        P("c", group),
        P("c", None),
    )
    return jax.shard_map(
        shards,
        mesh=grid,
        in_specs=placed,
        out_specs=(P("c", group), P("c", group)),
        check_vma=False,
    )
```

```python
import jax
import jax.numpy as jnp
from jax import lax
from jax.experimental import pallas as pl
from jax.experimental.pallas import tpu as pltpu
from jax.sharding import Mesh, PartitionSpec as P

F32 = jnp.float32
BF16 = jnp.bfloat16
I32 = jnp.int32
NY, NX, NZ = 4, 4, 8
ROWS = 2
PLANE = NY * NX * ROWS
OWN = NZ * PLANE
EARLY = OWN - PLANE
STEP = 32
TILE = 256
LANES = 128
VMEM = pl.BlockSpec(memory_space=pltpu.VMEM)
SHORT = pl.CostEstimate(flops=1024, bytes_accessed=1024, transcendentals=0)


def params():
    return pltpu.CompilerParams(vmem_limit_bytes=12 * 1024 * 1024)


def struct(shape, dtype):
    return jax.ShapeDtypeStruct(shape, dtype)


def call(body, out_shape, operands, scratch=()):
    several = isinstance(out_shape, tuple)
    return pl.pallas_call(
        body,
        out_shape=out_shape,
        in_specs=[VMEM] * len(operands),
        out_specs=(VMEM,) * len(out_shape) if several else VMEM,
        scratch_shapes=scratch,
        compiler_params=params(),
        cost_estimate=SHORT,
    )(*operands)


def up(n, k):
    return [(i, (i + k) % n) for i in range(n)]


def swap_cores(value):
    return lax.ppermute(value, "c", [(0, 1), (1, 0)])


def ring(block, axis, n):
    blocks = [block]
    from_low = from_high = block
    for _ in range(n // 2 - 1):
        from_low = lax.ppermute(from_low, axis, up(n, 1))
        from_high = lax.ppermute(from_high, axis, up(n, -1))
        blocks += [from_low, from_high]
    half = block.shape[0] // 2
    blocks.append(lax.ppermute(from_low[:half], axis, up(n, 1)))
    blocks.append(lax.ppermute(from_high[half:], axis, up(n, -1)))
    return blocks


def distance(position):
    return jnp.where(position % 2 == 1, NZ - (position + 1) // 2, position // 2)


def natural_row(row, z):
    position, inner = row // PLANE, row % PLANE
    y, x, i = inner // (NX * ROWS), inner // ROWS % NX, inner % ROWS
    return ((y * NX + x) * NZ + (z + distance(position)) % NZ) * ROWS + i


def iota(shape, axis):
    return lax.broadcasted_iota(I32, shape, axis)


def normalize(hidden, gain):
    values = hidden.astype(F32)
    spread = jnp.mean(values * values, axis=-1, keepdims=True)
    return (values * lax.rsqrt(spread + 1e-06) * gain.reshape(1, -1)).astype(BF16)


def student_norm_kernel(hidden_ref, gain_ref, out_ref):
    normed = normalize(hidden_ref[...], gain_ref[...])
    for peer in range(NY * NX):
        out_ref[peer] = normed


def student_norm(hidden, gain):
    return call(student_norm_kernel, struct((NY * NX, *hidden.shape), BF16), (hidden, gain))


def teacher_norm_kernel(hidden_ref, gain_ref, _, out_ref):
    z = lax.axis_index("z")
    normed = normalize(hidden_ref[...], gain_ref[...])
    n = normed.shape[0]
    row = iota((n, n), 0)
    position, x, i = row // (NX * ROWS), row // ROWS % NX, row % ROWS
    source = (x * NZ + (z + distance(position)) % NZ) * ROWS + i
    moved = jnp.where(iota((n, n), 1) == source, 1.0, 0.0).astype(BF16)
    out_ref[...] = jnp.dot(moved, normed, preferred_element_type=F32).astype(BF16)


def teacher_norm(hidden, gain, sent):
    return call(teacher_norm_kernel, struct(hidden.shape, BF16), (hidden, gain, sent))


def halves(ref_width):
    k, core = ref_width // 2, lax.axis_index("c")
    return tuple(pl.ds(pl.multiple_of(half * k, LANES), k) for half in (core, 1 - core))


def product(rows_ref, own_w_ref, other_w_ref, columns):
    own, other = halves(rows_ref.shape[1])
    return jnp.dot(
        rows_ref[:, own], own_w_ref[:, columns], preferred_element_type=F32
    ) + jnp.dot(rows_ref[:, other], other_w_ref[:, columns], preferred_element_type=F32)


def soft_cap(logits):
    return (30.0 * jnp.tanh(logits / 30.0)).astype(BF16)


def teacher_logits_kernel(b0, b1, b2, b3, b4, own_w_ref, other_w_ref, out_ref, rows_ref):
    section = b0.shape[0]
    y = lax.axis_index("y")
    row = iota((OWN, OWN), 0)
    position, inner = row // PLANE, row % PLANE
    apart = (inner // (NX * ROWS) - y) % NY
    place = jnp.where(apart == 0, 0, jnp.where(apart == NY - 1, 1, jnp.where(apart == 1, 2, 3)))
    source = place * section + position * (NX * ROWS) + inner % (NX * ROWS)
    moved = jnp.where(iota((OWN, OWN), 1) == source, 1.0, 0.0).astype(BF16)
    whole = jnp.concatenate([b0[...], b1[...], b2[...], b3[...], b4[...]])
    rows_ref[...] = jnp.dot(moved, whole, preferred_element_type=F32).astype(BF16)
    for at in range(0, out_ref.shape[1], TILE):
        columns = pl.ds(at, TILE)
        out_ref[:, columns] = soft_cap(product(rows_ref, own_w_ref, other_w_ref, columns))


def teacher_logits(blocks, own_head, other_head):
    k, vocab = own_head.shape
    out = struct((OWN, vocab), BF16)
    scratch = [pltpu.VMEM((OWN, 2 * k), BF16)]
    return call(teacher_logits_kernel, out, (*blocks, own_head, other_head), scratch)


def local_targets(targets_ref, z, first, rows):
    shape = (rows.shape[0], OWN)
    here = iota(shape, 1) == natural_row(rows, z)
    return jnp.sum(jnp.where(here, targets_ref[...], 0), axis=1, keepdims=True) - first


def first_column(vocab):
    y, x, z = lax.axis_index("y"), lax.axis_index("x"), lax.axis_index("z")
    return ((y * NX + x) * NZ + z) * vocab


def fold(values):
    total = values[:, :LANES]
    for start in range(LANES, values.shape[1], LANES):
        total = total + values[:, start : start + LANES]
    return total


def student_part(start, rows_ref, own_w_ref, other_w_ref, teacher_ref, targets_ref, capped_ref, write):
    n, vocab = capped_ref.shape
    for at in range(0, vocab, TILE):
        columns = pl.ds(at, TILE)
        capped_ref[:, columns] = soft_cap(product(rows_ref, own_w_ref, other_w_ref, columns))
    z, first = lax.axis_index("z"), first_column(vocab)
    for at in range(0, n, STEP):
        stud_vals = capped_ref[pl.ds(at, STEP)].astype(F32)
        teach_vals = teacher_ref[pl.ds(start + at, STEP)].astype(F32)
        stud_exp, teach_exp = jnp.exp(stud_vals), jnp.exp(teach_vals)
        target = local_targets(targets_ref, z, first, iota((STEP, 1), 0) + (start + at))
        hit = iota((STEP, vocab), 1) == target
        write(0, at, fold(teach_exp))
        write(1, at, fold(stud_exp))
        write(2, at, fold(teach_exp * (teach_vals - stud_vals)))
        write(3, at, fold(jnp.where(hit, stud_vals, 0.0)))


def early_kernel(*refs):
    *blocks, own_w_ref, other_w_ref, teacher_ref, targets_ref, capped_ref, sums_ref, rows_ref = refs

    def write(kind, at, value):
        sums_ref[kind, pl.ds(at, STEP)] = value

    for q, block in enumerate(blocks):
        rows_ref[pl.ds(q * PLANE, PLANE)] = block[...]
    student_part(0, rows_ref, own_w_ref, other_w_ref, teacher_ref, targets_ref, capped_ref, write)


def early_rows(planes, own_head, other_head, teacher, targets):
    k, vocab = own_head.shape
    out = (struct((EARLY, vocab), BF16), struct((4, EARLY, LANES), F32))
    scratch = [pltpu.VMEM((EARLY, 2 * k), BF16)]
    return call(early_kernel, out, (*planes, own_head, other_head, teacher, targets), scratch)


def last_kernel(
    low, high, own_w_ref, other_w_ref, teacher_ref, targets_ref, early_ref,
    capped_ref, out_ref, rows_ref, sums_ref,
):
    def write(kind, at, value):
        sums_ref[kind, pl.ds(EARLY + at, STEP)] = value

    rows_ref[...] = jnp.concatenate([low[...], high[...]])
    sums_ref[:, :EARLY] = early_ref[...]
    student_part(EARLY, rows_ref, own_w_ref, other_w_ref, teacher_ref, targets_ref, capped_ref, write)
    z = lax.axis_index("z")
    here = iota((OWN, OWN), 1) == natural_row(iota((OWN, OWN), 0), z)
    rows = []
    for kind in range(4):
        total = jnp.sum(sums_ref[kind], axis=1, keepdims=True)
        flat = jnp.sum(jnp.where(here, total, 0.0), axis=0, keepdims=True)
        rows += [flat[:, at : at + LANES] for at in range(0, OWN, LANES)]
    tile = jnp.concatenate(rows, axis=0)
    for peer in range(out_ref.shape[0]):
        out_ref[peer] = tile


def last_rows(low, high, own_head, other_head, teacher, targets, early):
    k, vocab = own_head.shape
    out = (struct((PLANE, vocab), BF16), struct((NY * NX, 8, LANES), F32))
    scratch = [pltpu.VMEM((PLANE, 2 * k), BF16), pltpu.VMEM((4, OWN, LANES), F32)]
    operands = (low, high, own_head, other_head, teacher, targets, early)
    return call(last_kernel, out, operands, scratch)


def spread_kernel(sums_ref, out_ref):
    total = sums_ref[0]
    for peer in range(1, sums_ref.shape[0]):
        total = total + sums_ref[peer]
    for peer in range(out_ref.shape[0]):
        out_ref[peer] = total


def spread(sums):
    return call(spread_kernel, struct((2 * NZ, 8, LANES), F32), (sums,))


def collect_kernel(early_ref, last_ref, teacher_ref, _, out_ref):
    out_ref[:EARLY] = early_ref[...]
    out_ref[EARLY:OWN] = last_ref[...]
    out_ref[OWN:] = teacher_ref[...]


def collect(early, last, teacher, sums):
    out = struct((2 * OWN, teacher.shape[1]), BF16)
    return call(collect_kernel, out, (early, last, teacher, sums))


def transpose_kernel(*refs):
    *blocks, low, high, _, keep_ref, send_ref, rows_ref = refs
    for q, block in enumerate(blocks):
        rows_ref[pl.ds(q * PLANE, PLANE)] = block[...]
    rows_ref[EARLY:] = jnp.concatenate([low[...], high[...]])
    k, core = keep_ref.shape[0], lax.axis_index("c")
    for ref, half in ((keep_ref, core), (send_ref, 1 - core)):
        for at in range(0, k, TILE):
            columns = pl.ds(pl.multiple_of(half * k + at, LANES), TILE)
            ref[pl.ds(at, TILE)] = rows_ref[:, columns].T


def transposed(blocks, sums):
    width = blocks[0].shape[1]
    out = struct((width // 2, OWN), BF16)
    scratch = [pltpu.VMEM((OWN, width), BF16)]
    return call(transpose_kernel, (out, out), (*blocks, sums), scratch)


def gradient_kernel(
    sums_ref, own_ref, other_ref, targets_ref, oth_targets_ref, own_rows, other_rows,
    loss_ref, out_ref, grad_ref,
):
    vocab = out_ref.shape[1]

    @pl.when(pl.program_id(0) == 0)
    def _():
        z, core = lax.axis_index("z"), lax.axis_index("c")
        first = first_column(vocab)
        position = (lax.axis_index("y") * NX + lax.axis_index("x")) * NZ + z
        here = iota((OWN, OWN), 1) == natural_row(iota((OWN, OWN), 0), z)
        totals = []
        for side in range(2):
            total = sums_ref[side]
            for peer in range(1, NZ):
                total = total + sums_ref[2 * peer + side]
            totals.append(total)
        own = jnp.where(core == 0, totals[0], totals[1])
        other = jnp.where(core == 0, totals[1], totals[0])

        def flat(tile, kind):
            return jnp.concatenate([tile[2 * kind : 2 * kind + 1], tile[2 * kind + 1 : 2 * kind + 2]], axis=1)

        teach_total, stud_total, cross_sum, target_logit = (flat(own, k) for k in range(4))
        loss = cross_sum / teach_total - jnp.log(teach_total) + 2.0 * jnp.log(stud_total) - target_logit
        lane = iota((1, OWN), 1)
        picked = [
            jnp.sum(jnp.where(lane == position * ROWS + i, loss, 0.0), axis=1, keepdims=True)
            for i in range(ROWS)
        ]
        loss_ref[...] = jnp.concatenate(picked, axis=1)

        for side, tile, values, targets in (
            (0, own, own_ref, targets_ref),
            (1, other, other_ref, oth_targets_ref),
        ):
            teach_scale = jnp.sum(jnp.where(here, 1.0 / flat(tile, 0), 0.0), axis=1, keepdims=True)
            stud_scale = jnp.sum(jnp.where(here, 2.0 / flat(tile, 1), 0.0), axis=1, keepdims=True)
            target = local_targets(targets, z, first, iota((OWN, 1), 0))
            for at in range(0, OWN, STEP):
                stud_vals = values[pl.ds(at, STEP)].astype(F32)
                teach_vals = values[pl.ds(OWN + at, STEP)].astype(F32)
                rows = slice(at, at + STEP)
                scaled = jnp.exp(stud_vals) * stud_scale[rows] - jnp.exp(teach_vals) * teach_scale[rows]
                hit = iota((STEP, vocab), 1) == target[rows]
                scaled = scaled - jnp.where(hit, 1.0, 0.0)
                value = scaled * (1.0 - stud_vals * stud_vals * (1.0 / 900.0))
                grad_ref[pl.ds(side * OWN + at, STEP)] = value.astype(BF16)

    tile = out_ref.shape[0]
    part = pl.ds(pl.multiple_of(pl.program_id(0) * tile, tile), tile)
    out_ref[...] = (
        jnp.dot(own_rows[part], grad_ref[:OWN], preferred_element_type=F32)
        + jnp.dot(other_rows[part], grad_ref[OWN:], preferred_element_type=F32)
    ).astype(BF16)


def gradient(sums, own, other, targets, oth_targets, own_rows, other_rows):
    k, vocab = own_rows.shape[0], own.shape[1]
    operands = [sums, own, other, targets, oth_targets, own_rows, other_rows]
    return pl.pallas_call(
        gradient_kernel,
        grid=(k // TILE,),
        out_shape=(struct((1, ROWS), F32), struct((k, vocab), BF16)),
        in_specs=[VMEM] * len(operands),
        out_specs=(
            pl.BlockSpec((1, ROWS), lambda j: (0, 0)),
            pl.BlockSpec((TILE, vocab), lambda j: (j, 0)),
        ),
        scratch_shapes=[pltpu.VMEM((2 * OWN, vocab), BF16)],
        compiler_params=params(),
        cost_estimate=SHORT,
    )(*operands)


def shards(
    student_hidden, teacher_hidden, student_gain, teacher_gain, student_head, teacher_head, targets
):
    sent = student_norm(student_hidden[0], student_gain)
    got = lax.all_to_all(sent, ("y", "x"), 0, 0, tiled=True)
    planes = ring(got.reshape(PLANE, got.shape[2]), "z", NZ)

    sections = ring(teacher_norm(teacher_hidden[0], teacher_gain, sent), "y", NY)

    other_teacher_head = swap_cores(teacher_head)
    other_student_head = swap_cores(student_head)
    oth_targets = swap_cores(targets)

    teacher = teacher_logits(sections, teacher_head, other_teacher_head)
    capped, early = early_rows(
        planes[: NZ - 1], student_head, other_student_head, teacher, targets
    )
    low, high = planes[NZ - 1 :]
    capped_last, sums = last_rows(
        low, high, student_head, other_student_head, teacher, targets, early
    )

    own = collect(capped, capped_last, teacher, sums)
    other = swap_cores(own)
    own_rows, sent_rows = transposed(planes, sums)
    other_rows = swap_cores(sent_rows)
    sums = lax.all_to_all(sums, ("y", "x"), 0, 0, tiled=True)
    sums = lax.all_to_all(spread(sums), ("z", "c"), 0, 0, tiled=True)
    return gradient(sums, own, other, targets, oth_targets, own_rows, other_rows)


def solution(mesh):
    cube = mesh.devices.reshape(NY, NX, NZ, 2)
    grid = Mesh(cube, ("y", "x", "z", "c"))
    group = ("y", "x", "z")
    placed = (
        P("c", group, None),
        P("c", "y", None),
        P(),
        P(),
        P("c", group),
        P("c", group),
        P("c", None),
    )
    return jax.shard_map(
        shards,
        mesh=grid,
        in_specs=placed,
        out_specs=(P("c", group), P("c", group)),
        check_vma=False,
    )
```

```python
import jax
import jax.numpy as jnp
from jax import lax
from jax.experimental import pallas as pl
from jax.experimental.pallas import tpu as pltpu
from jax.sharding import Mesh, PartitionSpec as P

F32 = jnp.float32
BF16 = jnp.bfloat16
I32 = jnp.int32
NY, NX, NZ = 4, 4, 8
ROWS = 2
PLANE = NY * NX * ROWS
OWN = NZ * PLANE
EARLY = OWN - PLANE
STEP = 32
TILE = 256
PARTS = 8
LANES = 128
VMEM = pl.BlockSpec(memory_space=pltpu.VMEM)
ANY = pl.BlockSpec(memory_space=pl.ANY)
SHORT = pl.CostEstimate(flops=1024, bytes_accessed=1024, transcendentals=0)
LONG = pl.CostEstimate(flops=5_000_000_000, bytes_accessed=1024, transcendentals=0)


def params(mebibytes=8):
    return pltpu.CompilerParams(vmem_limit_bytes=mebibytes * 1024 * 1024)


def struct(shape, dtype):
    return jax.ShapeDtypeStruct(shape, dtype)


def call(body, out_shape, operands, scratch=(), cost=SHORT):
    several = isinstance(out_shape, tuple)
    return pl.pallas_call(
        body,
        out_shape=out_shape,
        in_specs=[VMEM] * len(operands),
        out_specs=(VMEM,) * len(out_shape) if several else VMEM,
        scratch_shapes=scratch,
        compiler_params=params(),
        cost_estimate=cost,
    )(*operands)


def each(count, width, body):
    for index in range(count):
        body(index * width)


def up(n, k):
    return [(i, (i + k) % n) for i in range(n)]


def swap_cores(value):
    return lax.ppermute(value, "c", [(0, 1), (1, 0)])


def both_ways(low, high, axis, n):
    return lax.ppermute(low, axis, up(n, 1)), lax.ppermute(high, axis, up(n, -1))


def gate_kernel(low, high, t_low, t_high, *refs):
    low_out, high_out, t_low_out, t_high_out = refs[-4:]
    low_out[...] = low[...]
    high_out[...] = high[...]
    half = t_low_out.shape[0]
    t_low_out[...] = t_low[:half]
    t_high_out[...] = t_high[half:]


def gate(low, high, t_low, t_high, *others):
    part = struct((t_low.shape[0] // 2, t_low.shape[1]), BF16)
    plane = struct(low.shape, BF16)
    return pl.pallas_call(
        gate_kernel,
        out_shape=(plane, plane, part, part),
        in_specs=[VMEM] * 4 + [ANY] * len(others),
        out_specs=(VMEM,) * 4,
        compiler_params=params(4),
        cost_estimate=LONG,
    )(low, high, t_low, t_high, *others)


def rings(plane, rows, others):
    t_low, t_high = both_ways(rows, rows, "y", NY)
    planes = [plane]
    low = high = plane
    for step in range(NZ // 2 - 1):
        if step == 2:
            low, high, t_low_half, t_high_half = gate(low, high, t_low, t_high, *others)
        low, high = both_ways(low, high, "z", NZ)
        planes += [low, high]
    sections = [rows, t_low, t_high, *both_ways(t_low_half, t_high_half, "y", NY)]
    half = plane.shape[0] // 2
    planes += both_ways(low[:half], high[half:], "z", NZ)
    return planes, sections


def distance(position):
    return jnp.where(position % 2 == 1, NZ - (position + 1) // 2, position // 2)


def natural_row(row, z):
    position, inner = row // PLANE, row % PLANE
    y, x, i = inner // (NX * ROWS), inner // ROWS % NX, inner % ROWS
    return ((y * NX + x) * NZ + (z + distance(position)) % NZ) * ROWS + i


def iota(shape, axis):
    return lax.broadcasted_iota(I32, shape, axis)


def normalize(hidden, gain):
    values = hidden.astype(F32)
    spread = jnp.mean(values * values, axis=-1, keepdims=True)
    return (values * lax.rsqrt(spread + 1e-06) * gain.reshape(1, -1)).astype(BF16)


def peers_kernel(hidden_ref, out_ref):
    for peer in range(out_ref.shape[0]):
        out_ref[peer] = hidden_ref[...]


def for_peers(hidden):
    out = struct((NY * NX, *hidden.shape), BF16)
    return call(peers_kernel, out, (hidden,), cost=LONG)


def plane_kernel(*refs):
    got_ref, gain_ref, *_, out_ref, rows_ref = refs
    for peer in range(NY * NX):
        rows_ref[pl.ds(peer * ROWS, ROWS)] = got_ref[peer].astype(F32)
    out_ref[...] = normalize(rows_ref[...], gain_ref[...])


def plane_rows(got, gain, *others):
    shape = (PLANE, got.shape[2])
    return pl.pallas_call(
        plane_kernel,
        out_shape=struct(shape, BF16),
        in_specs=[VMEM, VMEM] + [ANY] * len(others),
        out_specs=VMEM,
        scratch_shapes=[pltpu.VMEM(shape, F32)],
        compiler_params=params(),
        cost_estimate=LONG,
    )(got, gain, *others)


def teacher_norm_kernel(hidden_ref, gain_ref, _, out_ref):
    z = lax.axis_index("z")
    normed = normalize(hidden_ref[...], gain_ref[...])
    n = normed.shape[0]
    row = iota((n, n), 0)
    position, x, i = row // (NX * ROWS), row // ROWS % NX, row % ROWS
    source = (x * NZ + (z + distance(position)) % NZ) * ROWS + i
    moved = jnp.where(iota((n, n), 1) == source, 1.0, 0.0).astype(BF16)
    out_ref[...] = jnp.dot(moved, normed, preferred_element_type=F32).astype(BF16)


def teacher_norm(hidden, gain, other):
    return pl.pallas_call(
        teacher_norm_kernel,
        out_shape=struct(hidden.shape, BF16),
        in_specs=[VMEM, VMEM, ANY],
        out_specs=VMEM,
        compiler_params=params(),
        cost_estimate=LONG,
    )(hidden, gain, other)


def halves(ref_width):
    k, core = ref_width // 2, lax.axis_index("c")
    return tuple(pl.ds(pl.multiple_of(half * k, LANES), k) for half in (core, 1 - core))


def fetch_kernel(head, out_ref, sem):
    part = head.shape[0] // PARTS
    copies = []
    for index in range(PARTS):
        rows = pl.ds(index * part, part)
        copies.append(pltpu.make_async_copy(head.at[rows], out_ref.at[rows], sem.at[index]))
        copies[-1].start()
    for copy in copies:
        copy.wait()


def fetched(head):
    return pl.pallas_call(
        fetch_kernel,
        out_shape=struct(head.shape, head.dtype),
        in_specs=[ANY],
        out_specs=VMEM,
        scratch_shapes=[pltpu.SemaphoreType.DMA((PARTS,))],
        compiler_params=params(4),
        cost_estimate=LONG,
    )(head)


def logits(rows_ref, own_w_ref, other_w_ref, out_ref):
    own, other = halves(rows_ref.shape[1])
    for at in range(0, out_ref.shape[1], TILE):
        columns = pl.ds(at, TILE)
        out_ref[:, columns] = soft_cap(
            jnp.dot(rows_ref[:, own], own_w_ref[:, columns], preferred_element_type=F32)
            + jnp.dot(rows_ref[:, other], other_w_ref[:, columns], preferred_element_type=F32)
        )


def soft_cap(logits):
    return (30.0 * jnp.tanh(logits / 30.0)).astype(BF16)


def near_teacher_kernel(b0, b1, b2, own_w_ref, other_w_ref, out_ref, rows_ref):
    rows_ref[...] = jnp.concatenate([b0[...], b1[...], b2[...]])
    logits(rows_ref, own_w_ref, other_w_ref, out_ref)


def near_teacher(blocks, own_head, other_head):
    k, vocab = own_head.shape
    n = 3 * blocks[0].shape[0]
    scratch = [pltpu.VMEM((n, 2 * k), BF16)]
    out = struct((n, vocab), BF16)
    return call(near_teacher_kernel, out, (*blocks, own_head, other_head), scratch, LONG)


def far_teacher_kernel(b3, b4, near_ref, own_w_ref, other_w_ref, out_ref, rows_ref, far_ref):
    rows_ref[...] = jnp.concatenate([b3[...], b4[...]])
    logits(rows_ref, own_w_ref, other_w_ref, far_ref)
    section = rows_ref.shape[0]
    y = lax.axis_index("y")
    row = iota((OWN, OWN), 0)
    position, inner = row // PLANE, row % PLANE
    apart = (inner // (NX * ROWS) - y) % NY
    place = jnp.where(apart == 0, 0, jnp.where(apart == NY - 1, 1, jnp.where(apart == 1, 2, 3)))
    source = place * section + position * (NX * ROWS) + inner % (NX * ROWS)
    moved = jnp.where(iota((OWN, OWN), 1) == source, 1.0, 0.0).astype(BF16)
    whole = jnp.concatenate([near_ref[...], far_ref[...]])
    out_ref[...] = jnp.dot(moved, whole, preferred_element_type=F32).astype(BF16)


def far_teacher(blocks, near, own_head, other_head):
    k, vocab = own_head.shape
    n = OWN - near.shape[0]
    scratch = [pltpu.VMEM((n, 2 * k), BF16), pltpu.VMEM((n, vocab), BF16)]
    out = struct((OWN, vocab), BF16)
    return call(far_teacher_kernel, out, (*blocks, near, own_head, other_head), scratch, LONG)


def local_targets(targets_ref, z, first, rows):
    shape = (rows.shape[0], OWN)
    here = iota(shape, 1) == natural_row(rows, z)
    return jnp.sum(jnp.where(here, targets_ref[...], 0), axis=1, keepdims=True) - first


def first_column(vocab):
    y, x, z = lax.axis_index("y"), lax.axis_index("x"), lax.axis_index("z")
    return ((y * NX + x) * NZ + z) * vocab


def fold(values):
    total = values[:, :LANES]
    for start in range(LANES, values.shape[1], LANES):
        total = total + values[:, start : start + LANES]
    return total


def sums_of(start, capped_ref, teacher_ref, targets_ref):
    n, vocab = capped_ref.shape
    z, first = lax.axis_index("z"), first_column(vocab)
    totals = [[] for _ in range(4)]
    for at in range(0, n, STEP):
        stud_vals = capped_ref[pl.ds(at, STEP)].astype(F32)
        teach_vals = teacher_ref[pl.ds(start + at, STEP)].astype(F32)
        stud_exp, teach_exp = jnp.exp(stud_vals), jnp.exp(teach_vals)
        target = local_targets(targets_ref, z, first, iota((STEP, 1), 0) + (start + at))
        hit = iota((STEP, vocab), 1) == target
        totals[0].append(fold(teach_exp))
        totals[1].append(fold(stud_exp))
        totals[2].append(fold(teach_exp * (teach_vals - stud_vals)))
        totals[3].append(fold(jnp.where(hit, stud_vals, 0.0)))
    here = iota((n, OWN), 1) == natural_row(iota((n, OWN), 0) + start, z)
    rows = []
    for parts in totals:
        total = jnp.sum(jnp.concatenate(parts, axis=0), axis=1, keepdims=True)
        flat = jnp.sum(jnp.where(here, total, 0.0), axis=0, keepdims=True)
        rows += [flat[:, at : at + LANES] for at in range(0, OWN, LANES)]
    return jnp.concatenate(rows, axis=0)


def early_kernel(*refs):
    *blocks, own_w_ref, other_w_ref, teacher_ref, targets_ref, capped_ref, sums_ref, rows_ref = refs
    for q, block in enumerate(blocks):
        rows_ref[pl.ds(q * PLANE, PLANE)] = block[...]
    logits(rows_ref, own_w_ref, other_w_ref, capped_ref)
    sums_ref[...] = sums_of(0, capped_ref, teacher_ref, targets_ref)


def early_rows(planes, own_head, other_head, teacher, targets):
    k, vocab = own_head.shape
    out = (struct((EARLY, vocab), BF16), struct((8, LANES), F32))
    scratch = [pltpu.VMEM((EARLY, 2 * k), BF16)]
    return call(early_kernel, out, (*planes, own_head, other_head, teacher, targets), scratch, LONG)


def last_kernel(
    low, high, own_w_ref, other_w_ref, teacher_ref, targets_ref, early_ref,
    capped_ref, out_ref, rows_ref,
):
    rows_ref[...] = jnp.concatenate([low[...], high[...]])
    logits(rows_ref, own_w_ref, other_w_ref, capped_ref)
    tile = early_ref[...] + sums_of(EARLY, capped_ref, teacher_ref, targets_ref)
    for peer in range(out_ref.shape[0]):
        out_ref[peer] = tile


def last_rows(low, high, own_head, other_head, teacher, targets, early):
    k, vocab = own_head.shape
    out = (struct((PLANE, vocab), BF16), struct((NY * NX, 8, LANES), F32))
    operands = (low, high, own_head, other_head, teacher, targets, early)
    return call(last_kernel, out, operands, [pltpu.VMEM((PLANE, 2 * k), BF16)])


def collect_kernel(early_ref, last_ref, teacher_ref, _, out_ref):
    out_ref[:EARLY] = early_ref[...]
    out_ref[EARLY:OWN] = last_ref[...]
    out_ref[OWN:] = teacher_ref[...]


def collect(early, last, teacher, sums):
    out = struct((2 * OWN, teacher.shape[1]), BF16)
    return call(collect_kernel, out, (early, last, teacher, sums))


def transpose_kernel(*refs):
    *blocks, low, high, _, keep_ref, send_ref, rows_ref = refs
    for q, block in enumerate(blocks):
        rows_ref[pl.ds(q * PLANE, PLANE)] = block[...]
    rows_ref[EARLY:] = jnp.concatenate([low[...], high[...]])
    k, core = keep_ref.shape[0], lax.axis_index("c")

    def turn(at):
        for ref, half in ((keep_ref, core), (send_ref, 1 - core)):
            columns = pl.ds(pl.multiple_of(half * k + at, LANES), TILE)
            ref[pl.ds(at, TILE)] = rows_ref[:, columns].T

    each(k // TILE, TILE, turn)


def transposed(blocks, sums):
    width = blocks[0].shape[1]
    out = struct((width // 2, OWN), BF16)
    scratch = [pltpu.VMEM((OWN, width), BF16)]
    return call(transpose_kernel, (out, out), (*blocks, sums), scratch)


def gradient_kernel(
    sums_ref, own_ref, other_ref, targets_ref, oth_targets_ref, own_rows, other_rows,
    loss_ref, out_ref, scale_ref, target_ref,
):
    vocab = own_ref.shape[1]

    @pl.when(pl.program_id(0) == 0)
    def _():
        z, core = lax.axis_index("z"), lax.axis_index("c")
        position = (lax.axis_index("y") * NX + lax.axis_index("x")) * NZ + z
        here = iota((OWN, OWN), 1) == natural_row(iota((OWN, OWN), 0), z)
        totals = []
        for side in range(2):
            total = sums_ref[side]
            for peer in range(1, NZ):
                total = total + sums_ref[2 * peer + side]
            totals.append(total)
        own = jnp.where(core == 0, totals[0], totals[1])
        other = jnp.where(core == 0, totals[1], totals[0])

        def flat(tile, kind):
            first, second = tile[2 * kind : 2 * kind + 1], tile[2 * kind + 1 : 2 * kind + 2]
            return jnp.concatenate([first, second], axis=1)

        teach_total, stud_total, cross_sum, target_logit = (flat(own, k) for k in range(4))
        loss = cross_sum / teach_total - jnp.log(teach_total) + 2.0 * jnp.log(stud_total) - target_logit
        lane = iota((1, OWN), 1)
        picked = [
            jnp.sum(jnp.where(lane == position * ROWS + i, loss, 0.0), axis=1, keepdims=True)
            for i in range(ROWS)
        ]
        loss_ref[...] = jnp.concatenate(picked, axis=1)
        first = first_column(vocab)
        for side, tile, targets in ((0, own, targets_ref), (1, other, oth_targets_ref)):
            rows = pl.ds(side * OWN, OWN)
            target = local_targets(targets, z, first, iota((OWN, 1), 0))
            target_ref[rows] = jnp.broadcast_to(target, (OWN, LANES))
            for kind, value in ((0, 1.0 / flat(tile, 0)), (1, 2.0 / flat(tile, 1))):
                column = jnp.sum(jnp.where(here, value, 0.0), axis=1, keepdims=True)
                scale_ref[kind, rows] = jnp.broadcast_to(column, (OWN, LANES))

    tile = out_ref.shape[1]
    start = pl.multiple_of(pl.program_id(0) * tile, tile)
    columns = pl.ds(start, tile)
    grads = []
    for side, values in ((0, own_ref), (1, other_ref)):
        rows = pl.ds(side * OWN, OWN)
        teach_scale, stud_scale = (scale_ref[kind, rows, :1] for kind in range(2))
        stud_vals = values[:OWN, columns].astype(F32)
        teach_vals = values[OWN:, columns].astype(F32)
        scaled = jnp.exp(stud_vals) * stud_scale - jnp.exp(teach_vals) * teach_scale
        hit = iota((OWN, tile), 1) == target_ref[rows, :1] - start
        scaled = scaled - jnp.where(hit, 1.0, 0.0)
        grads.append((scaled * (1.0 - stud_vals * stud_vals * (1.0 / 900.0))).astype(BF16))
    out_ref[...] = (
        jnp.dot(own_rows[...], grads[0], preferred_element_type=F32)
        + jnp.dot(other_rows[...], grads[1], preferred_element_type=F32)
    ).astype(BF16)


def gradient(sums, own, other, targets, oth_targets, own_rows, other_rows):
    k, vocab = own_rows.shape[0], own.shape[1]
    operands = [sums, own, other, targets, oth_targets, own_rows, other_rows]
    return pl.pallas_call(
        gradient_kernel,
        grid=(vocab // TILE,),
        out_shape=(struct((1, ROWS), F32), struct((k, vocab), BF16)),
        in_specs=[VMEM] * len(operands),
        out_specs=(
            pl.BlockSpec((1, ROWS), lambda j: (0, 0)),
            pl.BlockSpec((k, TILE), lambda j: (0, j)),
        ),
        scratch_shapes=[pltpu.VMEM((2, 2 * OWN, LANES), F32), pltpu.VMEM((2 * OWN, LANES), I32)],
        compiler_params=params(),
        cost_estimate=SHORT,
    )(*operands)


def shards(
    student_hidden, teacher_hidden, student_gain, teacher_gain, student_head, teacher_head, targets
):
    other_teacher_head = swap_cores(teacher_head)
    other_student_head = swap_cores(student_head)
    oth_targets = swap_cores(targets)

    sent = for_peers(student_hidden[0])
    got = lax.all_to_all(sent, ("y", "x"), 0, 0, tiled=True)
    teacher_rows = teacher_norm(teacher_hidden[0], teacher_gain, sent)
    waited = (teacher_rows, other_teacher_head, other_student_head, oth_targets)
    plane = plane_rows(got, student_gain, *waited)
    other_teacher_head, other_student_head = fetched(other_teacher_head), fetched(other_student_head)
    planes, sections = rings(plane, teacher_rows, (other_teacher_head, other_student_head))

    near = near_teacher(sections[:3], teacher_head, other_teacher_head)
    teacher = far_teacher(sections[3:], near, teacher_head, other_teacher_head)
    capped, early = early_rows(
        planes[: NZ - 1], student_head, other_student_head, teacher, targets
    )
    low, high = planes[NZ - 1 :]
    capped_last, sums = last_rows(
        low, high, student_head, other_student_head, teacher, targets, early
    )

    sums = jnp.sum(lax.all_to_all(sums, ("y", "x"), 0, 0, tiled=True), axis=0)
    sums = jnp.broadcast_to(sums[None], (2 * NZ, *sums.shape))
    own = collect(capped, capped_last, teacher, sums)
    other = swap_cores(own)
    own_rows, sent_rows = transposed(planes, sums)
    other_rows = swap_cores(sent_rows)
    sums = lax.all_to_all(sums, ("z", "c"), 0, 0, tiled=True)
    return gradient(sums, own, other, targets, oth_targets, own_rows, other_rows)


def solution(mesh):
    cube = mesh.devices.reshape(NY, NX, NZ, 2)
    grid = Mesh(cube, ("y", "x", "z", "c"))
    group = ("y", "x", "z")
    placed = (
        P("c", group, None),
        P("c", "y", None),
        P(),
        P(),
        P("c", group),
        P("c", group),
        P("c", None),
    )
    return jax.shard_map(
        shards,
        mesh=grid,
        in_specs=placed,
        out_specs=(P("c", group), P("c", group)),
        check_vma=False,
    )
```

```python
import jax
import jax.numpy as jnp
from jax import lax
from jax.experimental import pallas as pl
from jax.experimental.pallas import tpu as pltpu
from jax.sharding import Mesh, PartitionSpec as P

F32 = jnp.float32
BF16 = jnp.bfloat16
I32 = jnp.int32
NY, NX, NZ = 4, 4, 8
ROWS = 2
PLANE = NY * NX * ROWS
OWN = NZ * PLANE
EARLY = OWN - PLANE
STEP = 32
TILE = 256
PARTS = 8
LANES = 128
VMEM = pl.BlockSpec(memory_space=pltpu.VMEM)
ANY = pl.BlockSpec(memory_space=pl.ANY)
SHORT = pl.CostEstimate(flops=1024, bytes_accessed=1024, transcendentals=0)
LONG = pl.CostEstimate(flops=5_000_000_000, bytes_accessed=1024, transcendentals=0)


def params(mebibytes=8):
    return pltpu.CompilerParams(vmem_limit_bytes=mebibytes * 1024 * 1024)


def struct(shape, dtype):
    return jax.ShapeDtypeStruct(shape, dtype)


def call(body, out_shape, operands, scratch=(), cost=SHORT):
    several = isinstance(out_shape, tuple)
    return pl.pallas_call(
        body,
        out_shape=out_shape,
        in_specs=[VMEM] * len(operands),
        out_specs=(VMEM,) * len(out_shape) if several else VMEM,
        scratch_shapes=scratch,
        compiler_params=params(),
        cost_estimate=cost,
    )(*operands)


def each(count, width, body):
    for index in range(count):
        body(index * width)


def up(n, k):
    return [(i, (i + k) % n) for i in range(n)]


def swap_cores(value):
    return lax.ppermute(value, "c", [(0, 1), (1, 0)])


def both_ways(low, high, axis, n):
    return lax.ppermute(low, axis, up(n, 1)), lax.ppermute(high, axis, up(n, -1))


def gate_kernel(low, high, rows, t_low, t_high, *refs):
    low_out, high_out, t_low_out, t_high_out, near_out = refs[-5:]
    for index, block in enumerate((rows, t_low, t_high)):
        near_out[pl.ds(index * rows.shape[0], rows.shape[0])] = block[...]
    low_out[...] = low[...]
    high_out[...] = high[...]
    half = t_low_out.shape[0]
    t_low_out[...] = t_low[:half]
    t_high_out[...] = t_high[half:]


def gate(low, high, rows, t_low, t_high, *others):
    part = struct((t_low.shape[0] // 2, t_low.shape[1]), BF16)
    near = struct((3 * t_low.shape[0], t_low.shape[1]), BF16)
    plane = struct(low.shape, BF16)
    return pl.pallas_call(
        gate_kernel,
        out_shape=(plane, plane, part, part, near),
        in_specs=[VMEM] * 5 + [ANY] * len(others),
        out_specs=(VMEM,) * 5,
        compiler_params=params(4),
        cost_estimate=LONG,
    )(low, high, rows, t_low, t_high, *others)


def rings(plane, rows, others):
    t_low, t_high = both_ways(rows, rows, "y", NY)
    planes = [plane]
    low = high = plane
    for step in range(NZ // 2 - 1):
        if step == 2:
            low, high, t_low_half, t_high_half, near = gate(low, high, rows, t_low, t_high, *others)
        low, high = both_ways(low, high, "z", NZ)
        planes += [low, high]
    far = both_ways(t_low_half, t_high_half, "y", NY)
    half = plane.shape[0] // 2
    planes += both_ways(low[:half], high[half:], "z", NZ)
    return planes, near, far


def distance(position):
    return jnp.where(position % 2 == 1, NZ - (position + 1) // 2, position // 2)


def natural_row(row, z):
    position, inner = row // PLANE, row % PLANE
    y, x, i = inner // (NX * ROWS), inner // ROWS % NX, inner % ROWS
    return ((y * NX + x) * NZ + (z + distance(position)) % NZ) * ROWS + i


def iota(shape, axis):
    return lax.broadcasted_iota(I32, shape, axis)


def normalize(hidden, gain):
    values = hidden.astype(F32)
    spread = jnp.mean(values * values, axis=-1, keepdims=True)
    return (values * lax.rsqrt(spread + 1e-06) * gain.reshape(1, -1)).astype(BF16)


def peers_kernel(hidden_ref, out_ref):
    for peer in range(out_ref.shape[0]):
        out_ref[peer] = hidden_ref[...]


def for_peers(hidden):
    out = struct((NY * NX, *hidden.shape), BF16)
    return call(peers_kernel, out, (hidden,), cost=LONG)


def plane_kernel(*refs):
    got_ref, gain_ref, *_, out_ref, rows_ref = refs
    for peer in range(NY * NX):
        rows_ref[pl.ds(peer * ROWS, ROWS)] = got_ref[peer].astype(F32)
    out_ref[...] = normalize(rows_ref[...], gain_ref[...])


def plane_rows(got, gain, *others):
    shape = (PLANE, got.shape[2])
    return pl.pallas_call(
        plane_kernel,
        out_shape=struct(shape, BF16),
        in_specs=[VMEM, VMEM] + [ANY] * len(others),
        out_specs=VMEM,
        scratch_shapes=[pltpu.VMEM(shape, F32)],
        compiler_params=params(),
        cost_estimate=LONG,
    )(got, gain, *others)


def teacher_norm_kernel(hidden_ref, gain_ref, _, out_ref):
    z = lax.axis_index("z")
    normed = normalize(hidden_ref[...], gain_ref[...])
    n = normed.shape[0]
    row = iota((n, n), 0)
    position, x, i = row // (NX * ROWS), row // ROWS % NX, row % ROWS
    source = (x * NZ + (z + distance(position)) % NZ) * ROWS + i
    moved = jnp.where(iota((n, n), 1) == source, 1.0, 0.0).astype(BF16)
    out_ref[...] = jnp.dot(moved, normed, preferred_element_type=F32).astype(BF16)


def teacher_norm(hidden, gain, other):
    return pl.pallas_call(
        teacher_norm_kernel,
        out_shape=struct(hidden.shape, BF16),
        in_specs=[VMEM, VMEM, ANY],
        out_specs=VMEM,
        compiler_params=params(),
        cost_estimate=LONG,
    )(hidden, gain, other)


def halves(ref_width):
    k, core = ref_width // 2, lax.axis_index("c")
    return tuple(pl.ds(pl.multiple_of(half * k, LANES), k) for half in (core, 1 - core))


def fetch_kernel(head, out_ref, sem):
    part = head.shape[0] // PARTS
    copies = []
    for index in range(PARTS):
        rows = pl.ds(index * part, part)
        copies.append(pltpu.make_async_copy(head.at[rows], out_ref.at[rows], sem.at[index]))
        copies[-1].start()
    for copy in copies:
        copy.wait()


def fetched(head):
    return pl.pallas_call(
        fetch_kernel,
        out_shape=struct(head.shape, head.dtype),
        in_specs=[ANY],
        out_specs=VMEM,
        scratch_shapes=[pltpu.SemaphoreType.DMA((PARTS,))],
        compiler_params=params(4),
        cost_estimate=LONG,
    )(head)


def logits(rows_ref, own_w_ref, other_w_ref, out_ref):
    own, other = halves(rows_ref.shape[1])
    for at in range(0, out_ref.shape[1], TILE):
        columns = pl.ds(at, TILE)
        out_ref[:, columns] = soft_cap(
            jnp.dot(rows_ref[:, own], own_w_ref[:, columns], preferred_element_type=F32)
            + jnp.dot(rows_ref[:, other], other_w_ref[:, columns], preferred_element_type=F32)
        )


def soft_cap(logits):
    return (30.0 * jnp.tanh(logits / 30.0)).astype(BF16)


def near_teacher_kernel(rows_ref, own_w_ref, other_w_ref, out_ref):
    logits(rows_ref, own_w_ref, other_w_ref, out_ref)


def near_teacher(rows, own_head, other_head):
    out = struct((rows.shape[0], own_head.shape[1]), BF16)
    return call(near_teacher_kernel, out, (rows, own_head, other_head), cost=LONG)


def local_targets(targets_ref, z, first, rows):
    shape = (rows.shape[0], OWN)
    here = iota(shape, 1) == natural_row(rows, z)
    return jnp.sum(jnp.where(here, targets_ref[...], 0), axis=1, keepdims=True) - first


def first_column(vocab):
    y, x, z = lax.axis_index("y"), lax.axis_index("x"), lax.axis_index("z")
    return ((y * NX + x) * NZ + z) * vocab


def fold(values):
    total = values[:, :LANES]
    for start in range(LANES, values.shape[1], LANES):
        total = total + values[:, start : start + LANES]
    return total


def folded(totals):
    return [jnp.concatenate(parts, axis=0) if parts else None for parts in totals]


def tile_of(totals, start):
    z = lax.axis_index("z")
    rows = []
    for total in folded(totals):
        if total is None:
            flat = jnp.zeros((1, OWN), F32)
        else:
            n = total.shape[0]
            here = iota((n, OWN), 1) == natural_row(iota((n, OWN), 0) + start, z)
            column = jnp.sum(total, axis=1, keepdims=True)
            flat = jnp.sum(jnp.where(here, column, 0.0), axis=0, keepdims=True)
        rows += [flat[:, at : at + LANES] for at in range(0, OWN, LANES)]
    return jnp.concatenate(rows, axis=0)


def add_student(totals, start, capped_ref, targets_ref):
    n, vocab = capped_ref.shape
    z, first = lax.axis_index("z"), first_column(vocab)
    for at in range(0, n, STEP):
        stud_vals = capped_ref[pl.ds(at, STEP)].astype(F32)
        target = local_targets(targets_ref, z, first, iota((STEP, 1), 0) + (start + at))
        hit = iota((STEP, vocab), 1) == target
        totals[1].append(fold(jnp.exp(stud_vals)))
        totals[3].append(fold(jnp.where(hit, stud_vals, 0.0)))


def add_teacher(totals, start, stop, teacher_ref, capped_ref):
    for at in range(start, stop, STEP):
        teach_vals = teacher_ref[pl.ds(at, STEP)].astype(F32)
        teach_exp = jnp.exp(teach_vals)
        totals[0].append(fold(teach_exp))
        if at - start < capped_ref.shape[0]:
            stud_vals = capped_ref[pl.ds(at - start, STEP)].astype(F32)
            totals[2].append(fold(teach_exp * (teach_vals - stud_vals)))


def early_kernel(*refs):
    *blocks, own_w_ref, other_w_ref, targets_ref, capped_ref, sums_ref, rows_ref = refs
    for q, block in enumerate(blocks):
        rows_ref[pl.ds(q * PLANE, PLANE)] = block[...]
    logits(rows_ref, own_w_ref, other_w_ref, capped_ref)
    totals = [[], [], [], []]
    add_student(totals, 0, capped_ref, targets_ref)
    sums_ref[...] = tile_of(totals, 0)


def early_rows(planes, own_head, other_head, targets):
    k, vocab = own_head.shape
    out = (struct((EARLY, vocab), BF16), struct((8, LANES), F32))
    scratch = [pltpu.VMEM((EARLY, 2 * k), BF16)]
    return call(early_kernel, out, (*planes, own_head, other_head, targets), scratch, LONG)


def far_teacher_kernel(
    b3, b4, near_ref, own_w_ref, other_w_ref, capped_ref, early_ref,
    out_ref, sums_ref, rows_ref, far_ref,
):
    rows_ref[...] = jnp.concatenate([b3[...], b4[...]])
    logits(rows_ref, own_w_ref, other_w_ref, far_ref)
    section = rows_ref.shape[0]
    y = lax.axis_index("y")
    row = iota((OWN, OWN), 0)
    position, inner = row // PLANE, row % PLANE
    apart = (inner // (NX * ROWS) - y) % NY
    place = jnp.where(apart == 0, 0, jnp.where(apart == NY - 1, 1, jnp.where(apart == 1, 2, 3)))
    source = place * section + position * (NX * ROWS) + inner % (NX * ROWS)
    moved = jnp.where(iota((OWN, OWN), 1) == source, 1.0, 0.0).astype(BF16)
    whole = jnp.concatenate([near_ref[...], far_ref[...]])
    out_ref[...] = jnp.dot(moved, whole, preferred_element_type=F32).astype(BF16)
    totals = [[], [], [], []]
    add_teacher(totals, 0, EARLY, out_ref, capped_ref)
    sums_ref[...] = early_ref[...] + tile_of(totals, 0)


def far_teacher(blocks, near, own_head, other_head, capped, early):
    k, vocab = own_head.shape
    n = OWN - near.shape[0]
    scratch = [pltpu.VMEM((n, 2 * k), BF16), pltpu.VMEM((n, vocab), BF16)]
    out = (struct((OWN, vocab), BF16), struct((8, LANES), F32))
    operands = (*blocks, near, own_head, other_head, capped, early)
    return call(far_teacher_kernel, out, operands, scratch, LONG)


def last_kernel(
    low, high, own_w_ref, other_w_ref, teacher_ref, targets_ref, sums_ref,
    capped_ref, out_ref, rows_ref,
):
    rows_ref[...] = jnp.concatenate([low[...], high[...]])
    logits(rows_ref, own_w_ref, other_w_ref, capped_ref)
    totals = [[], [], [], []]
    add_student(totals, EARLY, capped_ref, targets_ref)
    add_teacher(totals, EARLY, OWN, teacher_ref, capped_ref)
    tile = sums_ref[...] + tile_of(totals, EARLY)
    for peer in range(out_ref.shape[0]):
        out_ref[peer] = tile


def last_rows(low, high, own_head, other_head, teacher, targets, sums):
    k, vocab = own_head.shape
    out = (struct((PLANE, vocab), BF16), struct((NY * NX, 8, LANES), F32))
    operands = (low, high, own_head, other_head, teacher, targets, sums)
    return call(last_kernel, out, operands, [pltpu.VMEM((PLANE, 2 * k), BF16)])


def collect_kernel(early_ref, last_ref, teacher_ref, _, out_ref):
    out_ref[:EARLY] = early_ref[...]
    out_ref[EARLY:OWN] = last_ref[...]
    out_ref[OWN:] = teacher_ref[...]


def collect(early, last, teacher, sums):
    out = struct((2 * OWN, teacher.shape[1]), BF16)
    return call(collect_kernel, out, (early, last, teacher, sums))


def transpose_kernel(*refs):
    *blocks, low, high, _, keep_ref, send_ref, rows_ref = refs
    for q, block in enumerate(blocks):
        rows_ref[pl.ds(q * PLANE, PLANE)] = block[...]
    rows_ref[EARLY:] = jnp.concatenate([low[...], high[...]])
    k, core = keep_ref.shape[0], lax.axis_index("c")

    def turn(at):
        for ref, half in ((keep_ref, core), (send_ref, 1 - core)):
            columns = pl.ds(pl.multiple_of(half * k + at, LANES), TILE)
            ref[pl.ds(at, TILE)] = rows_ref[:, columns].T

    each(k // TILE, TILE, turn)


def transposed(blocks, sums):
    width = blocks[0].shape[1]
    out = struct((width // 2, OWN), BF16)
    scratch = [pltpu.VMEM((OWN, width), BF16)]
    return call(transpose_kernel, (out, out), (*blocks, sums), scratch)


def gradient_kernel(
    sums_ref, own_ref, other_ref, targets_ref, oth_targets_ref, own_rows, other_rows,
    loss_ref, out, scale_ref, target_ref, grad_ref, out_ref, sems,
):
    vocab = own_ref.shape[1]

    z, core = lax.axis_index("z"), lax.axis_index("c")
    position = (lax.axis_index("y") * NX + lax.axis_index("x")) * NZ + z
    here = iota((OWN, OWN), 1) == natural_row(iota((OWN, OWN), 0), z)
    totals = []
    for side in range(2):
        total = sums_ref[side]
        for peer in range(1, NZ):
            total = total + sums_ref[2 * peer + side]
        totals.append(total)
    own = jnp.where(core == 0, totals[0], totals[1])
    other = jnp.where(core == 0, totals[1], totals[0])

    def flat(tile, kind):
        first, second = tile[2 * kind : 2 * kind + 1], tile[2 * kind + 1 : 2 * kind + 2]
        return jnp.concatenate([first, second], axis=1)

    teach_total, stud_total, cross_sum, target_logit = (flat(own, k) for k in range(4))
    loss = cross_sum / teach_total - jnp.log(teach_total) + 2.0 * jnp.log(stud_total) - target_logit
    lane = iota((1, OWN), 1)
    picked = [
        jnp.sum(jnp.where(lane == position * ROWS + i, loss, 0.0), axis=1, keepdims=True)
        for i in range(ROWS)
    ]
    loss_ref[...] = jnp.concatenate(picked, axis=1)
    first = first_column(vocab)
    for side, tile, targets in ((0, own, targets_ref), (1, other, oth_targets_ref)):
        rows = pl.ds(side * OWN, OWN)
        target = local_targets(targets, z, first, iota((OWN, 1), 0))
        target_ref[rows] = jnp.broadcast_to(target, (OWN, LANES))
        for kind, value in ((0, 1.0 / flat(tile, 0)), (1, 2.0 / flat(tile, 1))):
            column = jnp.sum(jnp.where(here, value, 0.0), axis=1, keepdims=True)
            scale_ref[kind, rows] = jnp.broadcast_to(column, (OWN, LANES))

    for start in range(0, vocab, TILE):
        columns = pl.ds(start, TILE)
        for side, values in ((0, own_ref), (1, other_ref)):
            rows = pl.ds(side * OWN, OWN)
            teach_scale, stud_scale = (scale_ref[kind, rows, :1] for kind in range(2))
            stud_vals = values[:OWN, columns].astype(F32)
            teach_vals = values[OWN:, columns].astype(F32)
            scaled = jnp.exp(stud_vals) * stud_scale - jnp.exp(teach_vals) * teach_scale
            hit = iota((OWN, TILE), 1) == target_ref[rows, :1] - start
            scaled = scaled - jnp.where(hit, 1.0, 0.0)
            value = scaled * (1.0 - stud_vals * stud_vals * (1.0 / 900.0))
            grad_ref[rows, columns] = value.astype(BF16)
    k = out_ref.shape[0]
    parts = [(0, k, start) for start in range(0, vocab - TILE, TILE)]
    parts += [(at, k // 2, vocab - TILE) for at in (0, k // 2)]
    copies = []
    for index, (at, count, start) in enumerate(parts):
        rows, columns = pl.ds(at, count), pl.ds(start, TILE)
        out_ref[rows, columns] = (
            jnp.dot(own_rows[rows], grad_ref[:OWN, columns], preferred_element_type=F32)
            + jnp.dot(other_rows[rows], grad_ref[OWN:, columns], preferred_element_type=F32)
        ).astype(BF16)
        copies.append(
            pltpu.make_async_copy(out_ref.at[rows, columns], out.at[rows, columns], sems.at[index])
        )
        copies[-1].start()
    for copy in copies:
        copy.wait()


def gradient(sums, own, other, targets, oth_targets, own_rows, other_rows):
    k, vocab = own_rows.shape[0], own.shape[1]
    operands = (sums, own, other, targets, oth_targets, own_rows, other_rows)
    return pl.pallas_call(
        gradient_kernel,
        out_shape=(struct((1, ROWS), F32), struct((k, vocab), BF16)),
        in_specs=[VMEM] * len(operands),
        out_specs=(VMEM, ANY),
        scratch_shapes=[
            pltpu.VMEM((2, 2 * OWN, LANES), F32),
            pltpu.VMEM((2 * OWN, LANES), I32),
            pltpu.VMEM((2 * OWN, vocab), BF16),
            pltpu.VMEM((k, vocab), BF16),
            pltpu.SemaphoreType.DMA((vocab // TILE + 1,)),
        ],
        compiler_params=params(12),
        cost_estimate=SHORT,
    )(*operands)


def shards(
    student_hidden, teacher_hidden, student_gain, teacher_gain, student_head, teacher_head, targets
):
    other_teacher_head = swap_cores(teacher_head)
    other_student_head = swap_cores(student_head)
    oth_targets = swap_cores(targets)

    sent = for_peers(student_hidden[0])
    got = lax.all_to_all(sent, ("y", "x"), 0, 0, tiled=True)
    teacher_rows = teacher_norm(teacher_hidden[0], teacher_gain, sent)
    waited = (teacher_rows, other_teacher_head, other_student_head, oth_targets)
    plane = plane_rows(got, student_gain, *waited)
    other_teacher_head, other_student_head = fetched(other_teacher_head), fetched(other_student_head)
    planes, near, far = rings(plane, teacher_rows, (other_teacher_head, other_student_head))

    near = near_teacher(near, teacher_head, other_teacher_head)
    capped, early = early_rows(planes[: NZ - 1], student_head, other_student_head, targets)
    teacher, early = far_teacher(far, near, teacher_head, other_teacher_head, capped, early)
    low, high = planes[NZ - 1 :]
    capped_last, sums = last_rows(
        low, high, student_head, other_student_head, teacher, targets, early
    )

    sums = jnp.sum(lax.all_to_all(sums, ("y", "x"), 0, 0, tiled=True), axis=0)
    sums = jnp.broadcast_to(sums[None], (2 * NZ, *sums.shape))
    own = collect(capped, capped_last, teacher, sums)
    other = swap_cores(own)
    own_rows, sent_rows = transposed(planes, sums)
    other_rows = swap_cores(sent_rows)
    sums = lax.all_to_all(sums, ("z", "c"), 0, 0, tiled=True)
    return gradient(sums, own, other, targets, oth_targets, own_rows, other_rows)


def solution(mesh):
    cube = mesh.devices.reshape(NY, NX, NZ, 2)
    grid = Mesh(cube, ("y", "x", "z", "c"))
    group = ("y", "x", "z")
    placed = (
        P("c", group, None),
        P("c", "y", None),
        P(),
        P(),
        P("c", group),
        P("c", group),
        P("c", None),
    )
    return jax.shard_map(
        shards,
        mesh=grid,
        in_specs=placed,
        out_specs=(P("c", group), P("c", group)),
        check_vma=False,
    )
```

```python
import jax
import jax.numpy as jnp
from jax import lax
from jax.experimental import pallas as pl
from jax.experimental.pallas import tpu as pltpu
from jax.sharding import Mesh, PartitionSpec as P

F32 = jnp.float32
BF16 = jnp.bfloat16
I32 = jnp.int32
NY, NX, NZ = 4, 4, 8
ROWS = 2
PLANE = NY * NX * ROWS
OWN = NZ * PLANE
EARLY = OWN - PLANE
STEP = 32
TILE = 256
PARTS = 8
LANES = 128
VMEM = pl.BlockSpec(memory_space=pltpu.VMEM)
ANY = pl.BlockSpec(memory_space=pl.ANY)
SHORT = pl.CostEstimate(flops=1024, bytes_accessed=1024, transcendentals=0)
LONG = pl.CostEstimate(flops=5_000_000_000, bytes_accessed=1024, transcendentals=0)


def params(mebibytes=8):
    return pltpu.CompilerParams(vmem_limit_bytes=mebibytes * 1024 * 1024)


def struct(shape, dtype):
    return jax.ShapeDtypeStruct(shape, dtype)


def call(body, out_shape, operands, scratch=(), cost=SHORT):
    several = isinstance(out_shape, tuple)
    return pl.pallas_call(
        body,
        out_shape=out_shape,
        in_specs=[VMEM] * len(operands),
        out_specs=(VMEM,) * len(out_shape) if several else VMEM,
        scratch_shapes=scratch,
        compiler_params=params(),
        cost_estimate=cost,
    )(*operands)


def each(count, width, body):
    for index in range(count):
        body(index * width)


def up(n, k):
    return [(i, (i + k) % n) for i in range(n)]


def swap_cores(value):
    return lax.ppermute(value, "c", [(0, 1), (1, 0)])


def both_ways(low, high, axis, n):
    return lax.ppermute(low, axis, up(n, 1)), lax.ppermute(high, axis, up(n, -1))


def gate_kernel(low, high, t_low, t_high, *refs):
    low_out, high_out, t_low_out, t_high_out = refs[-4:]
    low_out[...] = low[...]
    high_out[...] = high[...]
    half = t_low_out.shape[0]
    t_low_out[...] = t_low[:half]
    t_high_out[...] = t_high[half:]


def gate(low, high, t_low, t_high, *others):
    part = struct((t_low.shape[0] // 2, t_low.shape[1]), BF16)
    plane = struct(low.shape, BF16)
    return pl.pallas_call(
        gate_kernel,
        out_shape=(plane, plane, part, part),
        in_specs=[VMEM] * 4 + [ANY] * len(others),
        out_specs=(VMEM,) * 4,
        compiler_params=params(4),
        cost_estimate=LONG,
    )(low, high, t_low, t_high, *others)


def rings(plane, rows, teacher_head, other_teacher_head, other_student_head):
    t_low, t_high = both_ways(rows, rows, "y", NY)
    planes = [plane]
    low = high = plane
    for step in range(NZ // 2 - 1):
        if step == 2:
            near = near_teacher((rows, t_low, t_high), teacher_head, other_teacher_head)
            waited = (near, other_student_head)
            low, high, t_low_half, t_high_half = gate(low, high, t_low, t_high, *waited)
        low, high = both_ways(low, high, "z", NZ)
        planes += [low, high]
    far = both_ways(t_low_half, t_high_half, "y", NY)
    half = plane.shape[0] // 2
    planes += both_ways(low[:half], high[half:], "z", NZ)
    return planes, far, near


def distance(position):
    return jnp.where(position % 2 == 1, NZ - (position + 1) // 2, position // 2)


def natural_row(row, z):
    position, inner = row // PLANE, row % PLANE
    y, x, i = inner // (NX * ROWS), inner // ROWS % NX, inner % ROWS
    return ((y * NX + x) * NZ + (z + distance(position)) % NZ) * ROWS + i


def iota(shape, axis):
    return lax.broadcasted_iota(I32, shape, axis)


def normalize(hidden, gain):
    values = hidden.astype(F32)
    spread = jnp.mean(values * values, axis=-1, keepdims=True)
    return (values * lax.rsqrt(spread + 1e-06) * gain.reshape(1, -1)).astype(BF16)


def peers_kernel(hidden_ref, out_ref):
    for peer in range(out_ref.shape[0]):
        out_ref[peer] = hidden_ref[...]


def for_peers(hidden):
    out = struct((NY * NX, *hidden.shape), BF16)
    return call(peers_kernel, out, (hidden,), cost=LONG)


def plane_kernel(*refs):
    got_ref, gain_ref, *_, out_ref, rows_ref = refs
    for peer in range(NY * NX):
        rows_ref[pl.ds(peer * ROWS, ROWS)] = got_ref[peer].astype(F32)
    out_ref[...] = normalize(rows_ref[...], gain_ref[...])


def plane_rows(got, gain, *others):
    shape = (PLANE, got.shape[2])
    return pl.pallas_call(
        plane_kernel,
        out_shape=struct(shape, BF16),
        in_specs=[VMEM, VMEM] + [ANY] * len(others),
        out_specs=VMEM,
        scratch_shapes=[pltpu.VMEM(shape, F32)],
        compiler_params=params(),
        cost_estimate=LONG,
    )(got, gain, *others)


def teacher_norm_kernel(hidden_ref, gain_ref, _, out_ref):
    z = lax.axis_index("z")
    normed = normalize(hidden_ref[...], gain_ref[...])
    n = normed.shape[0]
    row = iota((n, n), 0)
    position, x, i = row // (NX * ROWS), row // ROWS % NX, row % ROWS
    source = (x * NZ + (z + distance(position)) % NZ) * ROWS + i
    moved = jnp.where(iota((n, n), 1) == source, 1.0, 0.0).astype(BF16)
    out_ref[...] = jnp.dot(moved, normed, preferred_element_type=F32).astype(BF16)


def teacher_norm(hidden, gain, other):
    return pl.pallas_call(
        teacher_norm_kernel,
        out_shape=struct(hidden.shape, BF16),
        in_specs=[VMEM, VMEM, ANY],
        out_specs=VMEM,
        compiler_params=params(),
        cost_estimate=LONG,
    )(hidden, gain, other)


def halves(ref_width):
    k, core = ref_width // 2, lax.axis_index("c")
    return tuple(pl.ds(pl.multiple_of(half * k, LANES), k) for half in (core, 1 - core))


def fetch_kernel(head, _, out_ref, sem):
    part = head.shape[0] // PARTS
    copies = []
    for index in range(PARTS):
        rows = pl.ds(index * part, part)
        copies.append(pltpu.make_async_copy(head.at[rows], out_ref.at[rows], sem.at[index]))
        copies[-1].start()
    for copy in copies:
        copy.wait()


def fetched(head, other):
    return pl.pallas_call(
        fetch_kernel,
        out_shape=struct(head.shape, head.dtype),
        in_specs=[ANY, ANY],
        out_specs=VMEM,
        scratch_shapes=[pltpu.SemaphoreType.DMA((PARTS,))],
        compiler_params=params(4),
        cost_estimate=LONG,
    )(head, other)


def logits(rows_ref, own_w_ref, other_w_ref, out_ref):
    own, other = halves(rows_ref.shape[1])
    for at in range(0, out_ref.shape[1], TILE):
        columns = pl.ds(at, TILE)
        out_ref[:, columns] = soft_cap(
            jnp.dot(rows_ref[:, own], own_w_ref[:, columns], preferred_element_type=F32)
            + jnp.dot(rows_ref[:, other], other_w_ref[:, columns], preferred_element_type=F32)
        )


def soft_cap(logits):
    return (30.0 * jnp.tanh(logits / 30.0)).astype(BF16)


def near_teacher_kernel(b0, b1, b2, own_w_ref, other_w_ref, out_ref, rows_ref):
    rows_ref[...] = jnp.concatenate([b0[...], b1[...], b2[...]])
    logits(rows_ref, own_w_ref, other_w_ref, out_ref)


def near_teacher(blocks, own_head, other_head):
    k, vocab = own_head.shape
    n = 3 * blocks[0].shape[0]
    scratch = [pltpu.VMEM((n, 2 * k), BF16)]
    out = struct((n, vocab), BF16)
    return call(near_teacher_kernel, out, (*blocks, own_head, other_head), scratch, LONG)


def local_targets(targets_ref, z, first, rows):
    shape = (rows.shape[0], OWN)
    here = iota(shape, 1) == natural_row(rows, z)
    return jnp.sum(jnp.where(here, targets_ref[...], 0), axis=1, keepdims=True) - first


def first_column(vocab):
    y, x, z = lax.axis_index("y"), lax.axis_index("x"), lax.axis_index("z")
    return ((y * NX + x) * NZ + z) * vocab


def fold(values):
    total = values[:, :LANES]
    for start in range(LANES, values.shape[1], LANES):
        total = total + values[:, start : start + LANES]
    return total


def folded(totals):
    return [jnp.concatenate(parts, axis=0) if parts else None for parts in totals]


def tile_of(totals, start):
    z = lax.axis_index("z")
    rows = []
    for total in folded(totals):
        if total is None:
            flat = jnp.zeros((1, OWN), F32)
        else:
            n = total.shape[0]
            here = iota((n, OWN), 1) == natural_row(iota((n, OWN), 0) + start, z)
            column = jnp.sum(total, axis=1, keepdims=True)
            flat = jnp.sum(jnp.where(here, column, 0.0), axis=0, keepdims=True)
        rows += [flat[:, at : at + LANES] for at in range(0, OWN, LANES)]
    return jnp.concatenate(rows, axis=0)


def add_student(totals, start, capped_ref, targets_ref):
    n, vocab = capped_ref.shape
    z, first = lax.axis_index("z"), first_column(vocab)
    for at in range(0, n, STEP):
        stud_vals = capped_ref[pl.ds(at, STEP)].astype(F32)
        target = local_targets(targets_ref, z, first, iota((STEP, 1), 0) + (start + at))
        hit = iota((STEP, vocab), 1) == target
        totals[1].append(fold(jnp.exp(stud_vals)))
        totals[3].append(fold(jnp.where(hit, stud_vals, 0.0)))


def add_teacher(totals, start, stop, teacher_ref, capped_ref):
    for at in range(start, stop, STEP):
        teach_vals = teacher_ref[pl.ds(at, STEP)].astype(F32)
        teach_exp = jnp.exp(teach_vals)
        totals[0].append(fold(teach_exp))
        if at - start < capped_ref.shape[0]:
            stud_vals = capped_ref[pl.ds(at - start, STEP)].astype(F32)
            totals[2].append(fold(teach_exp * (teach_vals - stud_vals)))


def early_kernel(*refs):
    *blocks, own_w_ref, other_w_ref, targets_ref, capped_ref, sums_ref, rows_ref = refs
    for q, block in enumerate(blocks):
        rows_ref[pl.ds(q * PLANE, PLANE)] = block[...]
    logits(rows_ref, own_w_ref, other_w_ref, capped_ref)
    totals = [[], [], [], []]
    add_student(totals, 0, capped_ref, targets_ref)
    sums_ref[...] = tile_of(totals, 0)


def early_rows(planes, own_head, other_head, targets):
    k, vocab = own_head.shape
    out = (struct((EARLY, vocab), BF16), struct((8, LANES), F32))
    scratch = [pltpu.VMEM((EARLY, 2 * k), BF16)]
    return call(early_kernel, out, (*planes, own_head, other_head, targets), scratch, LONG)


def far_teacher_kernel(
    b3, b4, near_ref, own_w_ref, other_w_ref, capped_ref, early_ref,
    out_ref, sums_ref, rows_ref, far_ref,
):
    rows_ref[...] = jnp.concatenate([b3[...], b4[...]])
    logits(rows_ref, own_w_ref, other_w_ref, far_ref)
    section = rows_ref.shape[0]
    y = lax.axis_index("y")
    row = iota((OWN, OWN), 0)
    position, inner = row // PLANE, row % PLANE
    apart = (inner // (NX * ROWS) - y) % NY
    place = jnp.where(apart == 0, 0, jnp.where(apart == NY - 1, 1, jnp.where(apart == 1, 2, 3)))
    source = place * section + position * (NX * ROWS) + inner % (NX * ROWS)
    moved = jnp.where(iota((OWN, OWN), 1) == source, 1.0, 0.0).astype(BF16)
    whole = jnp.concatenate([near_ref[...], far_ref[...]])
    out_ref[...] = jnp.dot(moved, whole, preferred_element_type=F32).astype(BF16)
    totals = [[], [], [], []]
    add_teacher(totals, 0, EARLY, out_ref, capped_ref)
    sums_ref[...] = early_ref[...] + tile_of(totals, 0)


def far_teacher(blocks, near, own_head, other_head, capped, early):
    k, vocab = own_head.shape
    n = OWN - near.shape[0]
    scratch = [pltpu.VMEM((n, 2 * k), BF16), pltpu.VMEM((n, vocab), BF16)]
    out = (struct((OWN, vocab), BF16), struct((8, LANES), F32))
    operands = (*blocks, near, own_head, other_head, capped, early)
    return call(far_teacher_kernel, out, operands, scratch, LONG)


def last_kernel(
    low, high, own_w_ref, other_w_ref, teacher_ref, targets_ref, sums_ref,
    capped_ref, out_ref, rows_ref,
):
    rows_ref[...] = jnp.concatenate([low[...], high[...]])
    logits(rows_ref, own_w_ref, other_w_ref, capped_ref)
    totals = [[], [], [], []]
    add_student(totals, EARLY, capped_ref, targets_ref)
    add_teacher(totals, EARLY, OWN, teacher_ref, capped_ref)
    tile = sums_ref[...] + tile_of(totals, EARLY)
    for peer in range(out_ref.shape[0]):
        out_ref[peer] = tile


def last_rows(low, high, own_head, other_head, teacher, targets, sums):
    k, vocab = own_head.shape
    out = (struct((PLANE, vocab), BF16), struct((NY * NX, 8, LANES), F32))
    operands = (low, high, own_head, other_head, teacher, targets, sums)
    return call(last_kernel, out, operands, [pltpu.VMEM((PLANE, 2 * k), BF16)])


def collect_kernel(early_ref, last_ref, teacher_ref, _, out_ref):
    out_ref[:EARLY] = early_ref[...]
    out_ref[EARLY:OWN] = last_ref[...]
    out_ref[OWN:] = teacher_ref[...]


def collect(early, last, teacher, sums):
    out = struct((2 * OWN, teacher.shape[1]), BF16)
    return call(collect_kernel, out, (early, last, teacher, sums))


def transpose_kernel(*refs):
    *blocks, low, high, _, keep_ref, send_ref, rows_ref = refs
    for q, block in enumerate(blocks):
        rows_ref[pl.ds(q * PLANE, PLANE)] = block[...]
    rows_ref[EARLY:] = jnp.concatenate([low[...], high[...]])
    k, core = keep_ref.shape[0], lax.axis_index("c")

    def turn(at):
        for ref, half in ((keep_ref, core), (send_ref, 1 - core)):
            columns = pl.ds(pl.multiple_of(half * k + at, LANES), TILE)
            ref[pl.ds(at, TILE)] = rows_ref[:, columns].T

    each(k // TILE, TILE, turn)


def transposed(blocks, sums):
    width = blocks[0].shape[1]
    out = struct((width // 2, OWN), BF16)
    scratch = [pltpu.VMEM((OWN, width), BF16)]
    return call(transpose_kernel, (out, out), (*blocks, sums), scratch)


def gradient_kernel(
    sums_ref, own_ref, other_ref, targets_ref, oth_targets_ref, own_rows, other_rows,
    loss_ref, out, scale_ref, target_ref, grad_ref, out_ref, sems,
):
    vocab = own_ref.shape[1]

    z, core = lax.axis_index("z"), lax.axis_index("c")
    position = (lax.axis_index("y") * NX + lax.axis_index("x")) * NZ + z
    here = iota((OWN, OWN), 1) == natural_row(iota((OWN, OWN), 0), z)
    totals = []
    for side in range(2):
        total = sums_ref[side]
        for peer in range(1, NZ):
            total = total + sums_ref[2 * peer + side]
        totals.append(total)
    own = jnp.where(core == 0, totals[0], totals[1])
    other = jnp.where(core == 0, totals[1], totals[0])

    def flat(tile, kind):
        first, second = tile[2 * kind : 2 * kind + 1], tile[2 * kind + 1 : 2 * kind + 2]
        return jnp.concatenate([first, second], axis=1)

    teach_total, stud_total, cross_sum, target_logit = (flat(own, k) for k in range(4))
    loss = cross_sum / teach_total - jnp.log(teach_total) + 2.0 * jnp.log(stud_total) - target_logit
    lane = iota((1, OWN), 1)
    picked = [
        jnp.sum(jnp.where(lane == position * ROWS + i, loss, 0.0), axis=1, keepdims=True)
        for i in range(ROWS)
    ]
    loss_ref[...] = jnp.concatenate(picked, axis=1)
    first = first_column(vocab)
    for side, tile, targets in ((0, own, targets_ref), (1, other, oth_targets_ref)):
        rows = pl.ds(side * OWN, OWN)
        target = local_targets(targets, z, first, iota((OWN, 1), 0))
        target_ref[rows] = jnp.broadcast_to(target, (OWN, LANES))
        for kind, value in ((0, 1.0 / flat(tile, 0)), (1, 2.0 / flat(tile, 1))):
            column = jnp.sum(jnp.where(here, value, 0.0), axis=1, keepdims=True)
            scale_ref[kind, rows] = jnp.broadcast_to(column, (OWN, LANES))

    for start in range(0, vocab, TILE):
        columns = pl.ds(start, TILE)
        for side, values in ((0, own_ref), (1, other_ref)):
            rows = pl.ds(side * OWN, OWN)
            teach_scale, stud_scale = (scale_ref[kind, rows, :1] for kind in range(2))
            stud_vals = values[:OWN, columns].astype(F32)
            teach_vals = values[OWN:, columns].astype(F32)
            scaled = jnp.exp(stud_vals) * stud_scale - jnp.exp(teach_vals) * teach_scale
            hit = iota((OWN, TILE), 1) == target_ref[rows, :1] - start
            scaled = scaled - jnp.where(hit, 1.0, 0.0)
            value = scaled * (1.0 - stud_vals * stud_vals * (1.0 / 900.0))
            grad_ref[rows, columns] = value.astype(BF16)
    k = out_ref.shape[0]
    parts = [(0, k, start) for start in range(0, vocab - TILE, TILE)]
    parts += [(at, k // 2, vocab - TILE) for at in (0, k // 2)]
    copies = []
    for index, (at, count, start) in enumerate(parts):
        rows, columns = pl.ds(at, count), pl.ds(start, TILE)
        out_ref[rows, columns] = (
            jnp.dot(own_rows[rows], grad_ref[:OWN, columns], preferred_element_type=F32)
            + jnp.dot(other_rows[rows], grad_ref[OWN:, columns], preferred_element_type=F32)
        ).astype(BF16)
        copies.append(
            pltpu.make_async_copy(out_ref.at[rows, columns], out.at[rows, columns], sems.at[index])
        )
        copies[-1].start()
    for copy in copies:
        copy.wait()


def gradient(sums, own, other, targets, oth_targets, own_rows, other_rows):
    k, vocab = own_rows.shape[0], own.shape[1]
    operands = (sums, own, other, targets, oth_targets, own_rows, other_rows)
    return pl.pallas_call(
        gradient_kernel,
        out_shape=(struct((1, ROWS), F32), struct((k, vocab), BF16)),
        in_specs=[VMEM] * len(operands),
        out_specs=(VMEM, ANY),
        scratch_shapes=[
            pltpu.VMEM((2, 2 * OWN, LANES), F32),
            pltpu.VMEM((2 * OWN, LANES), I32),
            pltpu.VMEM((2 * OWN, vocab), BF16),
            pltpu.VMEM((k, vocab), BF16),
            pltpu.SemaphoreType.DMA((vocab // TILE + 1,)),
        ],
        compiler_params=params(12),
        cost_estimate=SHORT,
    )(*operands)


def shards(
    student_hidden, teacher_hidden, student_gain, teacher_gain, student_head, teacher_head, targets
):
    other_teacher_head = swap_cores(teacher_head)
    other_student_head = swap_cores(student_head)
    oth_targets = swap_cores(targets)

    sent = for_peers(student_hidden[0])
    got = lax.all_to_all(sent, ("y", "x"), 0, 0, tiled=True)
    teacher_rows = teacher_norm(teacher_hidden[0], teacher_gain, sent)
    waited = (teacher_rows, other_teacher_head, other_student_head, oth_targets)
    plane = plane_rows(got, student_gain, *waited)
    other_teacher_head = fetched(other_teacher_head, plane)
    other_student_head = fetched(other_student_head, plane)
    planes, far, near = rings(
        plane, teacher_rows, teacher_head, other_teacher_head, other_student_head
    )

    capped, early = early_rows(planes[: NZ - 1], student_head, other_student_head, targets)
    teacher, early = far_teacher(far, near, teacher_head, other_teacher_head, capped, early)
    low, high = planes[NZ - 1 :]
    capped_last, sums = last_rows(
        low, high, student_head, other_student_head, teacher, targets, early
    )

    sums = jnp.sum(lax.all_to_all(sums, ("y", "x"), 0, 0, tiled=True), axis=0)
    sums = jnp.broadcast_to(sums[None], (2 * NZ, *sums.shape))
    own = collect(capped, capped_last, teacher, sums)
    other = swap_cores(own)
    own_rows, sent_rows = transposed(planes, sums)
    other_rows = swap_cores(sent_rows)
    sums = lax.all_to_all(sums, ("z", "c"), 0, 0, tiled=True)
    return gradient(sums, own, other, targets, oth_targets, own_rows, other_rows)


def solution(mesh):
    cube = mesh.devices.reshape(NY, NX, NZ, 2)
    grid = Mesh(cube, ("y", "x", "z", "c"))
    group = ("y", "x", "z")
    placed = (
        P("c", group, None),
        P("c", "y", None),
        P(),
        P(),
        P("c", group),
        P("c", group),
        P("c", None),
    )
    return jax.shard_map(
        shards,
        mesh=grid,
        in_specs=placed,
        out_specs=(P("c", group), P("c", group)),
        check_vma=False,
    )
```

```python
import jax
import jax.numpy as jnp
from jax import lax
from jax.experimental import pallas as pl
from jax.experimental.pallas import tpu as pltpu
from jax.sharding import Mesh, PartitionSpec as P

F32 = jnp.float32
BF16 = jnp.bfloat16
I32 = jnp.int32
NY, NX, NZ = 4, 4, 8
ROWS = 2
PLANE = NY * NX * ROWS
OWN = NZ * PLANE
EARLY = OWN - PLANE
STEP = 32
TILE = 256
PARTS = 8
LANES = 128
VMEM = pl.BlockSpec(memory_space=pltpu.VMEM)
ANY = pl.BlockSpec(memory_space=pl.ANY)
SHORT = pl.CostEstimate(flops=1024, bytes_accessed=1024, transcendentals=0)
LONG = pl.CostEstimate(flops=5_000_000_000, bytes_accessed=1024, transcendentals=0)


def params(mebibytes=8):
    return pltpu.CompilerParams(vmem_limit_bytes=mebibytes * 1024 * 1024)


def struct(shape, dtype):
    return jax.ShapeDtypeStruct(shape, dtype)


def call(body, out_shape, operands, scratch=(), cost=SHORT):
    several = isinstance(out_shape, tuple)
    return pl.pallas_call(
        body,
        out_shape=out_shape,
        in_specs=[VMEM] * len(operands),
        out_specs=(VMEM,) * len(out_shape) if several else VMEM,
        scratch_shapes=scratch,
        compiler_params=params(),
        cost_estimate=cost,
    )(*operands)


def each(count, width, body):
    for index in range(count):
        body(index * width)


def up(n, k):
    return [(i, (i + k) % n) for i in range(n)]


def swap_cores(value):
    return lax.ppermute(value, "c", [(0, 1), (1, 0)])


def both_ways(low, high, axis, n):
    return lax.ppermute(low, axis, up(n, 1)), lax.ppermute(high, axis, up(n, -1))


def gate_kernel(low, high, t_low, t_high, *refs):
    low_out, high_out, t_low_out, t_high_out = refs[-4:]
    low_out[...] = low[...]
    high_out[...] = high[...]
    half = t_low_out.shape[0]
    t_low_out[...] = t_low[:half]
    t_high_out[...] = t_high[half:]


def gate(low, high, t_low, t_high, *others):
    part = struct((t_low.shape[0] // 2, t_low.shape[1]), BF16)
    plane = struct(low.shape, BF16)
    return pl.pallas_call(
        gate_kernel,
        out_shape=(plane, plane, part, part),
        in_specs=[VMEM] * 4 + [ANY] * len(others),
        out_specs=(VMEM,) * 4,
        compiler_params=params(4),
        cost_estimate=LONG,
    )(low, high, t_low, t_high, *others)


def rings(plane, rows, teacher_head, other_teacher_head, other_student_head):
    t_low, t_high = both_ways(rows, rows, "y", NY)
    planes = [plane]
    low = high = plane
    for step in range(NZ // 2 - 1):
        if step == 2:
            other_student_head = fetched(other_student_head, planes[1])
            blocks = (rows, t_low, t_high)
            near = near_teacher(blocks, teacher_head, other_teacher_head, other_student_head)
            waited = (near, other_student_head)
            low, high, t_low_half, t_high_half = gate(low, high, t_low, t_high, *waited)
        low, high = both_ways(low, high, "z", NZ)
        planes += [low, high]
    far = both_ways(t_low_half, t_high_half, "y", NY)
    half = plane.shape[0] // 2
    planes += both_ways(low[:half], high[half:], "z", NZ)
    return planes, far, near, other_student_head


def distance(position):
    return jnp.where(position % 2 == 1, NZ - (position + 1) // 2, position // 2)


def natural_row(row, z):
    position, inner = row // PLANE, row % PLANE
    y, x, i = inner // (NX * ROWS), inner // ROWS % NX, inner % ROWS
    return ((y * NX + x) * NZ + (z + distance(position)) % NZ) * ROWS + i


def iota(shape, axis):
    return lax.broadcasted_iota(I32, shape, axis)


def normalize(hidden, gain):
    values = hidden.astype(F32)
    spread = jnp.mean(values * values, axis=-1, keepdims=True)
    return (values * lax.rsqrt(spread + 1e-06) * gain.reshape(1, -1)).astype(BF16)


def peers_kernel(hidden_ref, out_ref):
    for peer in range(out_ref.shape[0]):
        out_ref[peer] = hidden_ref[...]


def for_peers(hidden):
    out = struct((NY * NX, *hidden.shape), BF16)
    return call(peers_kernel, out, (hidden,), cost=LONG)


def plane_kernel(*refs):
    got_ref, gain_ref, *_, out_ref, rows_ref = refs
    for peer in range(NY * NX):
        rows_ref[pl.ds(peer * ROWS, ROWS)] = got_ref[peer].astype(F32)
    out_ref[...] = normalize(rows_ref[...], gain_ref[...])


def plane_rows(got, gain, *others):
    shape = (PLANE, got.shape[2])
    return pl.pallas_call(
        plane_kernel,
        out_shape=struct(shape, BF16),
        in_specs=[VMEM, VMEM] + [ANY] * len(others),
        out_specs=VMEM,
        scratch_shapes=[pltpu.VMEM(shape, F32)],
        compiler_params=params(),
        cost_estimate=LONG,
    )(got, gain, *others)


def teacher_norm_kernel(hidden_ref, gain_ref, _, out_ref):
    z = lax.axis_index("z")
    normed = normalize(hidden_ref[...], gain_ref[...])
    n = normed.shape[0]
    row = iota((n, n), 0)
    position, x, i = row // (NX * ROWS), row // ROWS % NX, row % ROWS
    source = (x * NZ + (z + distance(position)) % NZ) * ROWS + i
    moved = jnp.where(iota((n, n), 1) == source, 1.0, 0.0).astype(BF16)
    out_ref[...] = jnp.dot(moved, normed, preferred_element_type=F32).astype(BF16)


def teacher_norm(hidden, gain, other):
    return pl.pallas_call(
        teacher_norm_kernel,
        out_shape=struct(hidden.shape, BF16),
        in_specs=[VMEM, VMEM, ANY],
        out_specs=VMEM,
        compiler_params=params(),
        cost_estimate=LONG,
    )(hidden, gain, other)


def halves(ref_width):
    k, core = ref_width // 2, lax.axis_index("c")
    return tuple(pl.ds(pl.multiple_of(half * k, LANES), k) for half in (core, 1 - core))


def fetch_kernel(head, _, out_ref, sem):
    part = head.shape[0] // PARTS
    copies = []
    for index in range(PARTS):
        rows = pl.ds(index * part, part)
        copies.append(pltpu.make_async_copy(head.at[rows], out_ref.at[rows], sem.at[index]))
        copies[-1].start()
    for copy in copies:
        copy.wait()


def fetched(head, other):
    return pl.pallas_call(
        fetch_kernel,
        out_shape=struct(head.shape, head.dtype),
        in_specs=[ANY, ANY],
        out_specs=VMEM,
        scratch_shapes=[pltpu.SemaphoreType.DMA((PARTS,))],
        compiler_params=params(4),
        cost_estimate=LONG,
    )(head, other)


def logits(rows_ref, own_w_ref, other_w_ref, out_ref):
    own, other = halves(rows_ref.shape[1])
    for at in range(0, out_ref.shape[1], TILE):
        columns = pl.ds(at, TILE)
        out_ref[:, columns] = soft_cap(
            jnp.dot(rows_ref[:, own], own_w_ref[:, columns], preferred_element_type=F32)
            + jnp.dot(rows_ref[:, other], other_w_ref[:, columns], preferred_element_type=F32)
        )


def soft_cap(logits):
    return (30.0 * jnp.tanh(logits / 30.0)).astype(BF16)


def near_teacher_kernel(b0, b1, b2, own_w_ref, other_w_ref, _, out_ref, rows_ref):
    rows_ref[...] = jnp.concatenate([b0[...], b1[...], b2[...]])
    logits(rows_ref, own_w_ref, other_w_ref, out_ref)


def near_teacher(blocks, own_head, other_head, other):
    k, vocab = own_head.shape
    n = 3 * blocks[0].shape[0]
    scratch = [pltpu.VMEM((n, 2 * k), BF16)]
    out = struct((n, vocab), BF16)
    return call(near_teacher_kernel, out, (*blocks, own_head, other_head, other), scratch, LONG)


def local_targets(targets_ref, z, first, rows):
    shape = (rows.shape[0], OWN)
    here = iota(shape, 1) == natural_row(rows, z)
    return jnp.sum(jnp.where(here, targets_ref[...], 0), axis=1, keepdims=True) - first


def first_column(vocab):
    y, x, z = lax.axis_index("y"), lax.axis_index("x"), lax.axis_index("z")
    return ((y * NX + x) * NZ + z) * vocab


def fold(values):
    total = values[:, :LANES]
    for start in range(LANES, values.shape[1], LANES):
        total = total + values[:, start : start + LANES]
    return total


def folded(totals):
    return [jnp.concatenate(parts, axis=0) if parts else None for parts in totals]


def tile_of(totals, start):
    z = lax.axis_index("z")
    rows = []
    for total in folded(totals):
        if total is None:
            flat = jnp.zeros((1, OWN), F32)
        else:
            n = total.shape[0]
            here = iota((n, OWN), 1) == natural_row(iota((n, OWN), 0) + start, z)
            column = jnp.sum(total, axis=1, keepdims=True)
            flat = jnp.sum(jnp.where(here, column, 0.0), axis=0, keepdims=True)
        rows += [flat[:, at : at + LANES] for at in range(0, OWN, LANES)]
    return jnp.concatenate(rows, axis=0)


def add_student(totals, start, capped_ref, targets_ref):
    n, vocab = capped_ref.shape
    z, first = lax.axis_index("z"), first_column(vocab)
    for at in range(0, n, STEP):
        stud_vals = capped_ref[pl.ds(at, STEP)].astype(F32)
        target = local_targets(targets_ref, z, first, iota((STEP, 1), 0) + (start + at))
        hit = iota((STEP, vocab), 1) == target
        totals[1].append(fold(jnp.exp(stud_vals)))
        totals[3].append(fold(jnp.where(hit, stud_vals, 0.0)))


def add_teacher(totals, start, stop, teacher_ref, capped_ref):
    for at in range(start, stop, STEP):
        teach_vals = teacher_ref[pl.ds(at, STEP)].astype(F32)
        teach_exp = jnp.exp(teach_vals)
        totals[0].append(fold(teach_exp))
        if at - start < capped_ref.shape[0]:
            stud_vals = capped_ref[pl.ds(at - start, STEP)].astype(F32)
            totals[2].append(fold(teach_exp * (teach_vals - stud_vals)))


def early_kernel(*refs):
    *blocks, own_w_ref, other_w_ref, targets_ref, capped_ref, sums_ref, rows_ref = refs
    for q, block in enumerate(blocks):
        rows_ref[pl.ds(q * PLANE, PLANE)] = block[...]
    logits(rows_ref, own_w_ref, other_w_ref, capped_ref)
    totals = [[], [], [], []]
    add_student(totals, 0, capped_ref, targets_ref)
    sums_ref[...] = tile_of(totals, 0)


def early_rows(planes, own_head, other_head, targets):
    k, vocab = own_head.shape
    out = (struct((EARLY, vocab), BF16), struct((8, LANES), F32))
    scratch = [pltpu.VMEM((EARLY, 2 * k), BF16)]
    return call(early_kernel, out, (*planes, own_head, other_head, targets), scratch, LONG)


def far_teacher_kernel(
    b3, b4, near_ref, own_w_ref, other_w_ref, capped_ref, early_ref,
    out_ref, sums_ref, rows_ref, far_ref,
):
    rows_ref[...] = jnp.concatenate([b3[...], b4[...]])
    logits(rows_ref, own_w_ref, other_w_ref, far_ref)
    section = rows_ref.shape[0]
    y = lax.axis_index("y")
    row = iota((OWN, OWN), 0)
    position, inner = row // PLANE, row % PLANE
    apart = (inner // (NX * ROWS) - y) % NY
    place = jnp.where(apart == 0, 0, jnp.where(apart == NY - 1, 1, jnp.where(apart == 1, 2, 3)))
    source = place * section + position * (NX * ROWS) + inner % (NX * ROWS)
    moved = jnp.where(iota((OWN, OWN), 1) == source, 1.0, 0.0).astype(BF16)
    whole = jnp.concatenate([near_ref[...], far_ref[...]])
    out_ref[...] = jnp.dot(moved, whole, preferred_element_type=F32).astype(BF16)
    totals = [[], [], [], []]
    add_teacher(totals, 0, EARLY, out_ref, capped_ref)
    sums_ref[...] = early_ref[...] + tile_of(totals, 0)


def far_teacher(blocks, near, own_head, other_head, capped, early):
    k, vocab = own_head.shape
    n = OWN - near.shape[0]
    scratch = [pltpu.VMEM((n, 2 * k), BF16), pltpu.VMEM((n, vocab), BF16)]
    out = (struct((OWN, vocab), BF16), struct((8, LANES), F32))
    operands = (*blocks, near, own_head, other_head, capped, early)
    return call(far_teacher_kernel, out, operands, scratch, LONG)


def last_kernel(
    low, high, own_w_ref, other_w_ref, teacher_ref, targets_ref, sums_ref,
    capped_ref, out_ref, rows_ref,
):
    rows_ref[...] = jnp.concatenate([low[...], high[...]])
    logits(rows_ref, own_w_ref, other_w_ref, capped_ref)
    totals = [[], [], [], []]
    add_student(totals, EARLY, capped_ref, targets_ref)
    add_teacher(totals, EARLY, OWN, teacher_ref, capped_ref)
    tile = sums_ref[...] + tile_of(totals, EARLY)
    for peer in range(out_ref.shape[0]):
        out_ref[peer] = tile


def last_rows(low, high, own_head, other_head, teacher, targets, sums):
    k, vocab = own_head.shape
    out = (struct((PLANE, vocab), BF16), struct((NY * NX, 8, LANES), F32))
    operands = (low, high, own_head, other_head, teacher, targets, sums)
    return call(last_kernel, out, operands, [pltpu.VMEM((PLANE, 2 * k), BF16)])


def collect_kernel(early_ref, last_ref, teacher_ref, _, out_ref):
    out_ref[:EARLY] = early_ref[...]
    out_ref[EARLY:OWN] = last_ref[...]
    out_ref[OWN:] = teacher_ref[...]


def collect(early, last, teacher, sums):
    out = struct((2 * OWN, teacher.shape[1]), BF16)
    return call(collect_kernel, out, (early, last, teacher, sums))


def transpose_kernel(*refs):
    *blocks, low, high, _, keep_ref, send_ref, rows_ref = refs
    for q, block in enumerate(blocks):
        rows_ref[pl.ds(q * PLANE, PLANE)] = block[...]
    rows_ref[EARLY:] = jnp.concatenate([low[...], high[...]])
    k, core = keep_ref.shape[0], lax.axis_index("c")

    def turn(at):
        for ref, half in ((keep_ref, core), (send_ref, 1 - core)):
            columns = pl.ds(pl.multiple_of(half * k + at, LANES), TILE)
            ref[pl.ds(at, TILE)] = rows_ref[:, columns].T

    each(k // TILE, TILE, turn)


def transposed(blocks, sums):
    width = blocks[0].shape[1]
    out = struct((width // 2, OWN), BF16)
    scratch = [pltpu.VMEM((OWN, width), BF16)]
    return call(transpose_kernel, (out, out), (*blocks, sums), scratch)


def gradient_kernel(
    sums_ref, own_ref, other_ref, targets_ref, oth_targets_ref, own_rows, other_rows,
    loss_ref, out, scale_ref, target_ref, grad_ref, out_ref, sems,
):
    vocab = own_ref.shape[1]

    z, core = lax.axis_index("z"), lax.axis_index("c")
    position = (lax.axis_index("y") * NX + lax.axis_index("x")) * NZ + z
    here = iota((OWN, OWN), 1) == natural_row(iota((OWN, OWN), 0), z)
    totals = []
    for side in range(2):
        total = sums_ref[side]
        for peer in range(1, NZ):
            total = total + sums_ref[2 * peer + side]
        totals.append(total)
    own = jnp.where(core == 0, totals[0], totals[1])
    other = jnp.where(core == 0, totals[1], totals[0])

    def flat(tile, kind):
        first, second = tile[2 * kind : 2 * kind + 1], tile[2 * kind + 1 : 2 * kind + 2]
        return jnp.concatenate([first, second], axis=1)

    teach_total, stud_total, cross_sum, target_logit = (flat(own, k) for k in range(4))
    loss = cross_sum / teach_total - jnp.log(teach_total) + 2.0 * jnp.log(stud_total) - target_logit
    lane = iota((1, OWN), 1)
    picked = [
        jnp.sum(jnp.where(lane == position * ROWS + i, loss, 0.0), axis=1, keepdims=True)
        for i in range(ROWS)
    ]
    loss_ref[...] = jnp.concatenate(picked, axis=1)
    first = first_column(vocab)
    for side, tile, targets in ((0, own, targets_ref), (1, other, oth_targets_ref)):
        rows = pl.ds(side * OWN, OWN)
        target = local_targets(targets, z, first, iota((OWN, 1), 0))
        target_ref[rows] = jnp.broadcast_to(target, (OWN, LANES))
        for kind, value in ((0, 1.0 / flat(tile, 0)), (1, 2.0 / flat(tile, 1))):
            column = jnp.sum(jnp.where(here, value, 0.0), axis=1, keepdims=True)
            scale_ref[kind, rows] = jnp.broadcast_to(column, (OWN, LANES))

    for start in range(0, vocab, TILE):
        columns = pl.ds(start, TILE)
        for side, values in ((0, own_ref), (1, other_ref)):
            rows = pl.ds(side * OWN, OWN)
            teach_scale, stud_scale = (scale_ref[kind, rows, :1] for kind in range(2))
            stud_vals = values[:OWN, columns].astype(F32)
            teach_vals = values[OWN:, columns].astype(F32)
            scaled = jnp.exp(stud_vals) * stud_scale - jnp.exp(teach_vals) * teach_scale
            hit = iota((OWN, TILE), 1) == target_ref[rows, :1] - start
            scaled = scaled - jnp.where(hit, 1.0, 0.0)
            value = scaled * (1.0 - stud_vals * stud_vals * (1.0 / 900.0))
            grad_ref[rows, columns] = value.astype(BF16)
    k = out_ref.shape[0]
    parts = [(0, k, start) for start in range(0, vocab - TILE, TILE)]
    parts += [(at, k // 2, vocab - TILE) for at in (0, k // 2)]
    copies = []
    for index, (at, count, start) in enumerate(parts):
        rows, columns = pl.ds(at, count), pl.ds(start, TILE)
        out_ref[rows, columns] = (
            jnp.dot(own_rows[rows], grad_ref[:OWN, columns], preferred_element_type=F32)
            + jnp.dot(other_rows[rows], grad_ref[OWN:, columns], preferred_element_type=F32)
        ).astype(BF16)
        copies.append(
            pltpu.make_async_copy(out_ref.at[rows, columns], out.at[rows, columns], sems.at[index])
        )
        copies[-1].start()
    for copy in copies:
        copy.wait()


def gradient(sums, own, other, targets, oth_targets, own_rows, other_rows):
    k, vocab = own_rows.shape[0], own.shape[1]
    operands = (sums, own, other, targets, oth_targets, own_rows, other_rows)
    return pl.pallas_call(
        gradient_kernel,
        out_shape=(struct((1, ROWS), F32), struct((k, vocab), BF16)),
        in_specs=[VMEM] * len(operands),
        out_specs=(VMEM, ANY),
        scratch_shapes=[
            pltpu.VMEM((2, 2 * OWN, LANES), F32),
            pltpu.VMEM((2 * OWN, LANES), I32),
            pltpu.VMEM((2 * OWN, vocab), BF16),
            pltpu.VMEM((k, vocab), BF16),
            pltpu.SemaphoreType.DMA((vocab // TILE + 1,)),
        ],
        compiler_params=params(12),
        cost_estimate=SHORT,
    )(*operands)


def shards(
    student_hidden, teacher_hidden, student_gain, teacher_gain, student_head, teacher_head, targets
):
    other_teacher_head = swap_cores(teacher_head)
    other_student_head = swap_cores(student_head)
    oth_targets = swap_cores(targets)

    sent = for_peers(student_hidden[0])
    got = lax.all_to_all(sent, ("y", "x"), 0, 0, tiled=True)
    teacher_rows = teacher_norm(teacher_hidden[0], teacher_gain, sent)
    waited = (teacher_rows, other_teacher_head, other_student_head, oth_targets)
    plane = plane_rows(got, student_gain, *waited)
    other_teacher_head = fetched(other_teacher_head, plane)
    planes, far, near, other_student_head = rings(
        plane, teacher_rows, teacher_head, other_teacher_head, other_student_head
    )

    capped, early = early_rows(planes[: NZ - 1], student_head, other_student_head, targets)
    teacher, early = far_teacher(far, near, teacher_head, other_teacher_head, capped, early)
    low, high = planes[NZ - 1 :]
    capped_last, sums = last_rows(
        low, high, student_head, other_student_head, teacher, targets, early
    )

    sums = jnp.sum(lax.all_to_all(sums, ("y", "x"), 0, 0, tiled=True), axis=0)
    sums = jnp.broadcast_to(sums[None], (2 * NZ, *sums.shape))
    own = collect(capped, capped_last, teacher, sums)
    other = swap_cores(own)
    own_rows, sent_rows = transposed(planes, sums)
    other_rows = swap_cores(sent_rows)
    sums = lax.all_to_all(sums, ("z", "c"), 0, 0, tiled=True)
    return gradient(sums, own, other, targets, oth_targets, own_rows, other_rows)


def solution(mesh):
    cube = mesh.devices.reshape(NY, NX, NZ, 2)
    grid = Mesh(cube, ("y", "x", "z", "c"))
    group = ("y", "x", "z")
    placed = (
        P("c", group, None),
        P("c", "y", None),
        P(),
        P(),
        P("c", group),
        P("c", group),
        P("c", None),
    )
    return jax.shard_map(
        shards,
        mesh=grid,
        in_specs=placed,
        out_specs=(P("c", group), P("c", group)),
        check_vma=False,
    )
```
